32 devices in a mesh: head: 4 (over x, core), ctx: 8 (over z, y).
Axes of the slice: x: 2, y: 2, z: 4, core: 2. Of those that a mesh axis runs over, the one named last changes fastest.
Arguments:
- queries: bfloat16 [8192, 8192], P('ctx', 'head'), may hold values from -5 to 5
- keys: bfloat16 [8, 1024, 1024], P('ctx', 'head'), may hold values from -5 to 5
- values: bfloat16 [8, 1024, 1024], P('ctx', 'head'), may hold values from -6 to 6
- doc_ids: int32 [8192], P('ctx'), may hold values from 0 to 31, never falling along the last dimension, each value on 1 to 1024 neighbouring positions
- piece_owner: int32 [32], P('ctx'), may hold values from 0 to 7, as said below
Outputs:
- attended: bfloat16 [8192, 8192], P('ctx', 'head')
- owner_lse: float32 [8, 64, 2048], P('ctx', 'head')
The draws below stay inside these ranges and needn't reach their ends.
Inputs may be any that keep to these rules, and one draw needn't show every extreme that they name: `piece_owner`: entry s * 4 + j names the owner of piece j of index s; the 4 entries of one index are distinct, and one owner is named by every index.
All inputs are finite; a program needn't handle non-finite values.
Results may differ from the reference program's by a relative error of at most 0.0046.
Values may be sent and summed in bfloat16 or wider, within the bound.
No kernel may reach another device: no remote copies, remote signals or barrier semaphores. Data moves between devices by JAX's collectives and lax.ppermute only.
A program may use at most 64 MiB of HBM per device.

```python
import math
import jax
import jax.numpy as jnp
import numpy as np
from jax import lax

QUERY_HEADS = 64
KEY_VALUE_HEADS = 8
HEAD_SIZE = 128
TOKENS_PER_PART = 1024
MAXDOC = 1024
WINDOW_TOKENS = 8192
PIECE = 256
PIECES = 4
DOCS = 32
N_CTX = 8


def draw_queries(key, part):
    key = jax.random.fold_in(key, 1)
    base_offset = jnp.clip(jax.random.normal(key, (WINDOW_TOKENS, QUERY_HEADS, HEAD_SIZE), jnp.float32), -4.0, 4.0)
    return base_offset.reshape(WINDOW_TOKENS, QUERY_HEADS * HEAD_SIZE).astype(jnp.bfloat16)


def draw_keys(key, part):
    key = jax.random.fold_in(key, 2)
    base_offset = jnp.clip(jax.random.normal(key, (WINDOW_TOKENS, KEY_VALUE_HEADS, HEAD_SIZE), jnp.float32), -4.0, 4.0)
    return base_offset.reshape(N_CTX, TOKENS_PER_PART, KEY_VALUE_HEADS * HEAD_SIZE).astype(jnp.bfloat16)


def draw_piece_owner(key, part):
    key = jax.random.fold_in(key, 11)
    first, second, third, fourth = jax.random.split(key, 4)
    owners = jnp.arange(N_CTX, dtype=jnp.int32)
    busiest = jax.random.randint(first, (), 0, N_CTX)
    favour = jax.random.randint(second, (N_CTX,), 0, 4) * 300
    noise = jax.random.randint(third, (N_CTX, N_CTX), 0, 1000)
    score = jnp.where(owners[None, :] == busiest, 100000, noise + favour[None, :])
    score = score * N_CTX + owners[None, :]
    _, chosen = lax.top_k(score, PIECES)
    shuffle = jax.random.randint(fourth, (N_CTX, PIECES), 0, 1 << 16) * PIECES + jnp.arange(PIECES, dtype=jnp.int32)[None, :]
    order = jnp.argsort(shuffle, axis=1)
    chosen = jnp.take_along_axis(chosen, order, axis=1)
    return chosen.reshape(N_CTX * PIECES).astype(jnp.int32)


def level_of(own_key, shape, cuts, least, top_value):
    level, own = 1.0, jax.random.fold_in(own_key, 6)
    for dim, shards_of in cuts:
        heights = jnp.exp(jax.random.uniform(jax.random.fold_in(own, dim), (shards_of,), jnp.float32, least / len(cuts), top_value / len(cuts)))
        level = level * jnp.repeat(heights, shape[dim] // shards_of).reshape([-1 if axis == dim else 1 for axis in range(len(shape))])
    return level


def profile(count, total, most, skew):
    loads = [(1 << 20) // math.isqrt(grade ** skew) + 1 for grade in range(2, count + 1)]
    spare, holding = total - most - (count - 1), [1] * (count - 1)
    while spare > 0:
        free = [i for i in range(count - 1) if holding[i] < most]
        pool, left = sum([loads[i] for i in free]), spare
        for i in free:
            extra = min(most - holding[i], max(1, left * loads[i] // pool), spare)
            holding[i] = holding[i] + extra
            spare = spare - extra
    return np.array([most] + holding)


def uneven_parts(rng, number_of, total, limit, skew):
    if number_of == 2:
        one = jax.random.randint(rng, (), max(1, total - limit), min(limit, total - 1) + 1)
        return jnp.stack([one, total - one])
    tallies = jnp.asarray(profile(number_of, total, limit, skew), jnp.int32)
    couples = (number_of - 1) // 2
    donor, sink = tallies[1:1 + 2 * couples:2], tallies[2:2 + 2 * couples:2]
    margin = jnp.minimum(donor - 1, limit - sink)
    moved = jax.random.randint(jax.random.fold_in(rng, 1), (couples,), 0, 1 << 20) % (margin + 1)
    tallies = tallies.at[1:1 + 2 * couples:2].set(donor - moved).at[2:2 + 2 * couples:2].set(sink + moved)
    return tallies[jax.random.permutation(jax.random.fold_in(rng, 2), number_of)]


def centred(own_key, dims, deviation, reach, pieces=(), kind=jnp.bfloat16):
    entries = jax.random.normal(own_key, dims, jnp.float32) * deviation
    if len(pieces) > 0:
        entries = level_of(own_key, dims, pieces, -0.22, 0.18) * entries
    return jnp.clip(entries, min=-reach, max=reach).astype(kind)


def setup_inputs(seed: int = 0) -> dict:
    arg_keys = jax.random.split(jax.random.key(seed), 6)
    return {
        "queries": draw_queries(jax.random.fold_in(arg_keys[5], 71), 0),
        "keys": draw_keys(jax.random.fold_in(arg_keys[5], 71), 0),
        "values": centred(arg_keys[2], (N_CTX, TOKENS_PER_PART, KEY_VALUE_HEADS * HEAD_SIZE), 1.0, 6.0, ((0, 8), (1, 4))),
        "doc_ids": jnp.searchsorted(jnp.cumsum(uneven_parts(arg_keys[3], DOCS, WINDOW_TOKENS, MAXDOC, 2)), jnp.arange(WINDOW_TOKENS), side="right").astype(jnp.int32),
        "piece_owner": draw_piece_owner(jax.random.fold_in(arg_keys[5], 71), 0),
    }


NEG = -1e30


def reference(queries, keys, values, doc_ids, piece_owner):
    share_amount = QUERY_HEADS // KEY_VALUE_HEADS
    block_rows = math.gcd(256, WINDOW_TOKENS)
    span_length = MAXDOC + block_rows
    key_block_rows = jnp.concatenate([jnp.zeros((span_length, KEY_VALUE_HEADS, HEAD_SIZE), jnp.bfloat16), keys.reshape(WINDOW_TOKENS, KEY_VALUE_HEADS, HEAD_SIZE)])
    value_block_rows = jnp.concatenate([jnp.zeros((span_length, KEY_VALUE_HEADS, HEAD_SIZE), jnp.bfloat16), values.reshape(WINDOW_TOKENS, KEY_VALUE_HEADS, HEAD_SIZE)])
    docs = jnp.concatenate([jnp.full((span_length,), -1, jnp.int32), doc_ids])

    def one_block(index):
        start_position = index * block_rows
        query_block_rows = lax.dynamic_slice_in_dim(queries, start_position, block_rows, 0).reshape(block_rows, KEY_VALUE_HEADS, share_amount, HEAD_SIZE)
        window_keys = lax.dynamic_slice_in_dim(key_block_rows, start_position + block_rows, span_length, 0)
        window_values = lax.dynamic_slice_in_dim(value_block_rows, start_position + block_rows, span_length, 0)
        window_docs = lax.dynamic_slice_in_dim(docs, start_position + block_rows, span_length, 0)
        key_pos = start_position + block_rows - span_length + jnp.arange(span_length, dtype=jnp.int32)
        query_pos = start_position + jnp.arange(block_rows, dtype=jnp.int32)
        query_docs = lax.dynamic_slice_in_dim(doc_ids, start_position, block_rows, 0)
        allowed = (window_docs[None, :] == query_docs[:, None]) & (key_pos[None, :] <= query_pos[:, None])
        scores = jnp.einsum("pksd,tkd->kspt", query_block_rows.astype(jnp.float32), window_keys.astype(jnp.float32)) * (HEAD_SIZE ** -0.5)
        scores = jnp.where(allowed[None, None], scores, NEG)
        top = jnp.max(scores, axis=-1, keepdims=True)
        prob = jnp.exp(scores - top)
        total = jnp.sum(prob, axis=-1, keepdims=True)
        weights = (prob / total).astype(jnp.bfloat16)
        mixed = jnp.einsum("kspt,tkd->pksd", weights.astype(jnp.float32), window_values.astype(jnp.float32))
        lse = (top + jnp.log(total))[..., 0]
        return mixed.astype(jnp.bfloat16).reshape(block_rows, QUERY_HEADS * HEAD_SIZE), lse.reshape(QUERY_HEADS, block_rows).T

    outs, lses = lax.map(one_block, jnp.arange(WINDOW_TOKENS // block_rows, dtype=jnp.int32))
    attended = outs.reshape(WINDOW_TOKENS, QUERY_HEADS * HEAD_SIZE)
    lse_pieces = lses.reshape(N_CTX, PIECES, PIECE, QUERY_HEADS)
    owner_table = (piece_owner.reshape(N_CTX, PIECES)[:, :, None] == jnp.arange(N_CTX, dtype=jnp.int32)[None, None, :]).astype(jnp.float32)
    owner_lse = jnp.einsum("sco,scph->ohsp", owner_table, lse_pieces, precision=lax.Precision.HIGHEST)
    return attended, owner_lse.reshape(N_CTX, QUERY_HEADS, N_CTX * PIECE)
```

```python
import functools
import math

import jax
import jax.numpy as jnp
from jax import lax
from jax.experimental import pallas as pl
from jax.experimental.pallas import tpu as pltpu
from jax.sharding import PartitionSpec as P

HEAD = 128
BLOCK = 256
NEG = -1e30
SCALE2 = HEAD ** (-0.5) * math.log2(math.e)
LN2 = math.log(2.0)
VMEM_LIMIT = 48 * 1024 * 1024
NT = (((1,), (1,)), ((), ()))


def f32_dot(a, b, dims):
    return lax.dot_general(a, b, dims, preferred_element_type=jnp.float32)


def eye_rows(column):
    rows = column.shape[0]
    eye = lax.broadcasted_iota(jnp.int32, (HEAD, HEAD), 0) == lax.broadcasted_iota(jnp.int32, (HEAD, HEAD), 1)
    parts = [
        jnp.sum(jnp.where(eye, column[i : i + HEAD], 0.0), axis=0, keepdims=True) for i in range(0, rows, HEAD)
    ]
    return jnp.concatenate(parts, axis=1)


def row_column(row):
    return jnp.broadcast_to(row, (HEAD, row.shape[1])).T


def prep_kernel(k_ref, v_ref, ko_ref, vo_ref):
    size, _, width = ko_ref.shape
    for i in range(size):
        ko_ref[i] = k_ref[0, :, i * width : (i + 1) * width]
        vo_ref[i] = v_ref[0, :, i * width : (i + 1) * width]


def prep(keys, values, size):
    _, rows, cols = keys.shape
    shape = jax.ShapeDtypeStruct((size, rows, cols // size), keys.dtype)
    return pl.pallas_call(
        prep_kernel,
        out_shape=(shape, shape),
        cost_estimate=pl.CostEstimate(flops=0, bytes_accessed=4 * keys.size * 2, transcendentals=0),
    )(keys, values)


def own_kernel(first_ref, q_ref, k_ref, v_ref, docs_ref, o_ref, l_ref, vx_ref, bias_ref):
    turn = pl.program_id(1)
    share = q_ref.shape[1] // HEAD
    blocks = k_ref.shape[0] // BLOCK

    @pl.when(turn == 0)
    def _():
        vx_ref[:, :HEAD] = v_ref[...]
        vx_ref[:, HEAD:] = jnp.ones(v_ref.shape, v_ref.dtype)

    first = first_ref[turn]
    for n in range(1, blocks + 1):

        @pl.when(turn - first + 1 == n)
        def _(n=n):
            width = n * BLOCK
            base = pl.multiple_of(first * BLOCK, BLOCK)
            here = pl.multiple_of(turn * BLOCK, BLOCK)
            q_docs = row_column(docs_ref[:, pl.ds(here, BLOCK)])
            k_docs = docs_ref[:, pl.ds(base, width)]
            q_docs = jnp.concatenate([q_docs] * (width // HEAD), axis=1)
            ahead = lax.broadcasted_iota(jnp.int32, (BLOCK, width), 1) - lax.broadcasted_iota(
                jnp.int32, (BLOCK, width), 0
            )
            keep = (q_docs == k_docs) & (ahead <= width - BLOCK)
            bias_ref[:, :width] = jnp.where(keep, 0.0, NEG)
            k = k_ref[pl.ds(base, width), :]
            vx = vx_ref[pl.ds(base, width), :]
            for h in range(share):
                cols = slice(h * HEAD, (h + 1) * HEAD)
                s = f32_dot(q_ref[:, cols], k, NT) * SCALE2 + bias_ref[:, :width]
                top = jnp.max(s, axis=1, keepdims=True)
                p = jnp.exp2(s - top).astype(jnp.bfloat16)
                got = f32_dot(p, vx, (((1,), (0,)), ((), ())))
                total = got[:, HEAD:]
                o_ref[:, cols] = (got[:, :HEAD] / total).astype(o_ref.dtype)
                l_ref[h : h + 1, :] = eye_rows(top + jnp.log2(total))


def own_part(first, queries, k, v, docs):
    tok, width = queries.shape
    groups = k.shape[1] // HEAD
    share = width // HEAD // groups
    turns = tok // BLOCK
    spec = pltpu.PrefetchScalarGridSpec(
        num_scalar_prefetch=1,
        grid=(groups, turns),
        in_specs=[
            pl.BlockSpec((BLOCK, share * HEAD), lambda g, t, f: (t, g)),
            pl.BlockSpec((tok, HEAD), lambda g, t, f: (0, g)),
            pl.BlockSpec((tok, HEAD), lambda g, t, f: (0, g)),
            pl.BlockSpec((1, tok), lambda g, t, f: (0, 0)),
        ],
        out_specs=[
            pl.BlockSpec((BLOCK, share * HEAD), lambda g, t, f: (t, g)),
            pl.BlockSpec((share, BLOCK), lambda g, t, f: (g, t)),
        ],
        scratch_shapes=[
            pltpu.VMEM((tok, 2 * HEAD), jnp.bfloat16),
            pltpu.VMEM((BLOCK, tok), jnp.float32),
        ],
    )
    return pl.pallas_call(
        own_kernel,
        grid_spec=spec,
        out_shape=(
            jax.ShapeDtypeStruct((tok, width), jnp.bfloat16),
            jax.ShapeDtypeStruct((groups * share, tok), jnp.float32),
        ),
        compiler_params=pltpu.CompilerParams(vmem_limit_bytes=VMEM_LIMIT),
        cost_estimate=pl.CostEstimate(
            flops=2 * tok * tok * width, bytes_accessed=4 * tok * width, transcendentals=tok * tok * width // HEAD // 2
        ),
    )(first, queries, k, v, docs)


def lse_kernel(meta_ref, owner_ref, q_ref, k_ref, lown_ref, l_ref, send_ref):
    group, turn = pl.program_id(0), pl.program_id(1)
    share = q_ref.shape[1] // HEAD
    tok = k_ref.shape[0]
    blocks = tok // BLOCK
    ahead, behind = meta_ref[0], meta_ref[1]
    steps = meta_ref[2]
    rows = pl.multiple_of(group * share, share)

    @pl.when((group == 0) & (turn == 0))
    def _():
        l_ref[...] = lown_ref[...]

    for n in range(1, blocks + 1):

        @pl.when((turn < steps) & ((ahead + BLOCK - 1) // BLOCK == n))
        def _(n=n):
            width = n * BLOCK
            k = k_ref[tok - width :, :]
            place = lax.broadcasted_iota(jnp.int32, (1, width), 1)
            bias = jnp.where(place >= width - ahead, 0.0, NEG)
            here = pl.multiple_of(turn * BLOCK, BLOCK)
            found = []
            for h in range(share):
                s = f32_dot(q_ref[:, h * HEAD : (h + 1) * HEAD], k, NT) * SCALE2 + bias
                top = jnp.max(s, axis=1, keepdims=True)
                total = jnp.sum(jnp.exp2(s - top), axis=1, keepdims=True)
                found.append(eye_rows(jnp.broadcast_to(top + jnp.log2(total), (BLOCK, HEAD))))
            new = jnp.concatenate(found, axis=0)
            old = lown_ref[pl.ds(rows, share), pl.ds(here, BLOCK)]
            most = jnp.maximum(new, old)
            both = most + jnp.log2(jnp.exp2(new - most) + jnp.exp2(old - most))
            token = here + lax.broadcasted_iota(jnp.int32, (share, BLOCK), 1)
            l_ref[pl.ds(rows, share), pl.ds(here, BLOCK)] = jnp.where(token < behind, both, old)

    @pl.when((group == pl.num_programs(0) - 1) & (turn == pl.num_programs(1) - 1))
    def _():
        owners, _, piece = send_ref.shape
        for o in range(owners):
            found = jnp.zeros(send_ref.shape[1:], jnp.float32)
            for j in range(tok // piece):
                part = l_ref[:, j * piece : (j + 1) * piece] * LN2
                found = jnp.where(owner_ref[j] == o, part, found)
            send_ref[o] = found


def lse_part(meta, owner, queries, k, lown, owners, piece):
    tok, width = queries.shape
    heads = width // HEAD
    groups = k.shape[1] // HEAD
    share = heads // groups
    spec = pltpu.PrefetchScalarGridSpec(
        num_scalar_prefetch=2,
        grid=(groups, tok // BLOCK),
        in_specs=[
            pl.BlockSpec((BLOCK, share * HEAD), lambda g, t, m, o: (jnp.minimum(t, jnp.maximum(m[2] - 1, 0)), g)),
            pl.BlockSpec((tok, HEAD), lambda g, t, m, o: (0, g)),
            pl.BlockSpec((heads, tok), lambda g, t, m, o: (0, 0)),
        ],
        out_specs=[
            pl.BlockSpec((heads, tok), lambda g, t, m, o: (0, 0)),
            pl.BlockSpec((owners, heads, piece), lambda g, t, m, o: (0, 0, 0)),
        ],
    )
    return pl.pallas_call(
        lse_kernel,
        grid_spec=spec,
        out_shape=(
            jax.ShapeDtypeStruct((heads, tok), jnp.float32),
            jax.ShapeDtypeStruct((owners, heads, piece), jnp.float32),
        ),
        compiler_params=pltpu.CompilerParams(vmem_limit_bytes=VMEM_LIMIT),
        cost_estimate=pl.CostEstimate(
            flops=tok * tok * width // 2, bytes_accessed=2 * tok * width, transcendentals=tok * tok * heads // 4
        ),
    )(meta, owner, queries, k, lown)


def rest_kernel(meta_ref, q_ref, k_ref, v_ref, lown_ref, l_ref, old_ref, o_ref):
    turn = pl.program_id(1)
    share = q_ref.shape[1] // HEAD
    tok = k_ref.shape[0]
    blocks = tok // BLOCK
    ahead, behind, steps = meta_ref[0], meta_ref[1], meta_ref[2]

    @pl.when((steps == 0) & (turn == 0))
    def _():
        o_ref[...] = old_ref[...]

    for n in range(1, blocks + 1):

        @pl.when((turn < steps) & ((ahead + BLOCK - 1) // BLOCK == n))
        def _(n=n):
            width = n * BLOCK
            k = k_ref[tok - width :, :]
            v = v_ref[tok - width :, :]
            place = lax.broadcasted_iota(jnp.int32, (1, width), 1)
            bias = jnp.where(place >= width - ahead, 0.0, NEG)
            token = turn * BLOCK + lax.broadcasted_iota(jnp.int32, (BLOCK, HEAD), 0)
            inside = token < behind
            for h in range(share):
                cols = slice(h * HEAD, (h + 1) * HEAD)
                final = row_column(l_ref[h : h + 1, :])
                kept = jnp.exp2(row_column(lown_ref[h : h + 1, :]) - final)
                s = f32_dot(q_ref[:, cols], k, NT) * SCALE2 + bias
                p = jnp.exp2(jnp.minimum(s - jnp.concatenate([final] * (width // HEAD), axis=1), 1.0))
                got = f32_dot(p.astype(jnp.bfloat16), v, (((1,), (0,)), ((), ())))
                old = old_ref[:, cols].astype(jnp.float32)
                o_ref[:, cols] = jnp.where(inside, old * kept + got, old).astype(o_ref.dtype)


def rest_part(meta, queries, k, v, lown, lfull, done):
    tok, width = queries.shape
    heads = width // HEAD
    groups = k.shape[1] // HEAD
    share = heads // groups

    def tile(t, m):
        return jnp.minimum(t, jnp.maximum(m[2] - 1, 0))

    spec = pltpu.PrefetchScalarGridSpec(
        num_scalar_prefetch=1,
        grid=(groups, tok // BLOCK),
        in_specs=[
            pl.BlockSpec((BLOCK, share * HEAD), lambda g, t, m: (tile(t, m), g)),
            pl.BlockSpec((tok, HEAD), lambda g, t, m: (0, g)),
            pl.BlockSpec((tok, HEAD), lambda g, t, m: (0, g)),
            pl.BlockSpec((share, BLOCK), lambda g, t, m: (g, tile(t, m))),
            pl.BlockSpec((share, BLOCK), lambda g, t, m: (g, tile(t, m))),
            pl.BlockSpec((BLOCK, share * HEAD), lambda g, t, m: (tile(t, m), g)),
        ],
        out_specs=pl.BlockSpec((BLOCK, share * HEAD), lambda g, t, m: (tile(t, m), g)),
    )
    return pl.pallas_call(
        rest_kernel,
        grid_spec=spec,
        out_shape=jax.ShapeDtypeStruct((tok, width), jnp.bfloat16),
        input_output_aliases={6: 0},
        compiler_params=pltpu.CompilerParams(vmem_limit_bytes=VMEM_LIMIT),
        cost_estimate=pl.CostEstimate(
            flops=tok * tok * width, bytes_accessed=4 * tok * width, transcendentals=tok * tok * heads // 4
        ),
    )(meta, queries, k, v, lown, lfull, done)


def spread_kernel(x_ref, o_ref):
    owners, _, piece = x_ref.shape
    for i in range(owners):
        o_ref[0, :, i * piece : (i + 1) * piece] = x_ref[i]


def spread(got):
    owners, heads, piece = got.shape
    return pl.pallas_call(
        spread_kernel,
        out_shape=jax.ShapeDtypeStruct((1, heads, owners * piece), got.dtype),
        cost_estimate=pl.CostEstimate(flops=0, bytes_accessed=8 * got.size, transcendentals=0),
    )(got)


def passed_along(block, axis):
    return lax.ppermute(block, axis, [(i, i + 1) for i in range(lax.axis_size(axis) - 1)])


def per_device(queries, keys, values, doc_ids, piece_owner):
    ctx_size, head_size = lax.axis_size("ctx"), lax.axis_size("head")
    mine = lax.axis_index("ctx")
    tok, width = queries.shape
    piece = 2 * tok // ctx_size
    cols = keys.shape[2] // head_size

    k_send, v_send = prep(keys, values, head_size)
    k_own = lax.all_to_all(k_send, "head", 0, 0, tiled=True)
    v_own = lax.all_to_all(v_send, "head", 0, 0, tiled=True)
    k_old = passed_along(k_own, "ctx").reshape(tok, cols)
    v_old = passed_along(v_own, "ctx").reshape(tok, cols)
    k_own, v_own = k_own.reshape(tok, cols), v_own.reshape(tok, cols)

    all_docs = lax.all_gather(doc_ids, "ctx", tiled=True)
    starts = doc_ids[::BLOCK]
    first = jnp.sum((doc_ids[None, :] < starts[:, None]).astype(jnp.int32), axis=1) // BLOCK
    earlier = jnp.arange(all_docs.shape[0], dtype=jnp.int32) < mine * tok
    ahead = jnp.sum((earlier & (all_docs == doc_ids[0])).astype(jnp.int32))
    behind = jnp.sum((doc_ids == doc_ids[0]).astype(jnp.int32))
    steps = jnp.where(ahead > 0, -(-behind // BLOCK), 0)
    meta = jnp.stack([ahead, behind, steps])

    done, lown = own_part(first, queries, k_own, v_own, doc_ids.reshape(1, tok))
    lfull, send = lse_part(meta, piece_owner, queries, k_old, lown, ctx_size, piece)
    got = lax.all_to_all(send, "ctx", 0, 0, tiled=True)
    attended = rest_part(meta, queries, k_old, v_old, lown, lfull, done)
    return attended, spread(got)


def solution(mesh):
    return jax.shard_map(
        per_device,
        mesh=mesh,
        in_specs=(
            P("ctx", "head"),
            P("ctx", "head", None),
            P("ctx", "head", None),
            P("ctx"),
            P("ctx"),
        ),
        out_specs=(P("ctx", "head"), P("ctx", "head", None)),
        check_vma=False,
    )
```

```python
import math

import jax
import jax.numpy as jnp
from jax import lax
from jax.experimental import pallas as pl
from jax.experimental.pallas import tpu as pltpu
from jax.sharding import PartitionSpec as P

HEAD = 128
BLOCK = 256
INFO = 16
CODE = 32
NEG = -1e30
SCALE2 = HEAD ** (-0.5) * math.log2(math.e)
LN2 = math.log(2.0)
VMEM_LIMIT = 57 * 1024 * 1024
NT = (((1,), (1,)), ((), ()))
NN = (((1,), (0,)), ((), ()))
IN_VMEM = pl.BlockSpec(memory_space=pltpu.VMEM)
IN_SMEM = pl.BlockSpec(memory_space=pltpu.SMEM)
IN_HBM = pl.BlockSpec(memory_space=pltpu.HBM)


def f32_dot(a, b, dims):
    return lax.dot_general(a, b, dims, preferred_element_type=jnp.float32)


def eye_rows(column):
    eye = lax.broadcasted_iota(jnp.int32, (HEAD, HEAD), 0) == lax.broadcasted_iota(jnp.int32, (HEAD, HEAD), 1)
    parts = [
        jnp.sum(jnp.where(eye, column[i : i + HEAD], 0.0), axis=0, keepdims=True)
        for i in range(0, column.shape[0], HEAD)
    ]
    return jnp.concatenate(parts, axis=1)


def row_column(row):
    return jnp.broadcast_to(row, (HEAD, row.shape[1])).T


def count(flags):
    return jnp.sum(flags.astype(jnp.int32))


def tile_of(ref, turn):
    return ref.at[pl.ds(pl.multiple_of(turn * BLOCK, BLOCK), BLOCK), :]


def prep_kernel(size, k_ref, v_ref, docs_ref, own_ref, *next_refs):
    here = lax.axis_index("head")
    rows, cols = k_ref.shape[1], k_ref.shape[2] // size
    for j in range(size):
        own_ref[j, :rows] = k_ref[0, :, j * cols : (j + 1) * cols]
        own_ref[j, rows:] = v_ref[0, :, j * cols : (j + 1) * cols]
    docs = docs_ref[...]
    last = docs[:, docs.shape[1] - 1 :]
    run = jnp.sum(jnp.where(docs == last, 1.0, 0.0), axis=1, keepdims=True)
    high = jnp.floor(run * (1.0 / CODE))
    line = lax.broadcasted_iota(jnp.int32, (INFO, cols), 0)
    info = jnp.where(line == 0, last.astype(jnp.float32), jnp.where(line == 1, high, run - high * CODE))
    info = info.astype(k_ref.dtype)
    for m in range(size):
        start = pl.multiple_of(lax.rem(here + m, size) * cols, cols)
        next_refs[m][:rows] = k_ref[0, :, pl.ds(start, cols)]
        next_refs[m][rows : 2 * rows] = v_ref[0, :, pl.ds(start, cols)]
        next_refs[m][2 * rows :] = info


def prep(keys, values, docs, size):
    _, rows, width = keys.shape
    cols = width // size
    own = jax.ShapeDtypeStruct((size, 2 * rows, cols), keys.dtype)
    onward = jax.ShapeDtypeStruct((2 * rows + INFO, cols), keys.dtype)

    def kernel(*refs):
        prep_kernel(size, *refs)

    return pl.pallas_call(
        kernel,
        out_shape=(own,) + (onward,) * size,
        in_specs=[IN_VMEM] * 3,
        out_specs=(IN_VMEM,) * (size + 1),
        cost_estimate=pl.CostEstimate(flops=0, bytes_accessed=12 * keys.size, transcendentals=0),
    )(keys, values, docs)


def own_kernel(q_hbm, kv_ref, docs_ref, o_hbm, l_ref, q_ref, o_ref, k_ref, vx_ref, bias_ref, q_sem, o_sem):
    parts, rows, cols = kv_ref.shape[0], kv_ref.shape[1] // 2, kv_ref.shape[2]
    groups = cols // HEAD
    turns = q_ref.shape[0]
    share = q_ref.shape[2] // HEAD // groups

    def q_copy(turn):
        return pltpu.make_async_copy(tile_of(q_hbm, turn), q_ref.at[turn], q_sem.at[turn])

    def o_copy(turn):
        return pltpu.make_async_copy(o_ref.at[turn], tile_of(o_hbm, turn), o_sem.at[turn])

    for turn in range(turns):
        q_copy(turn).start()
    for j in range(parts):
        k_ref[j * rows : (j + 1) * rows] = kv_ref[j, :rows]
        for g in range(groups):
            vx_ref[g, j * rows : (j + 1) * rows, :HEAD] = kv_ref[j, rows:, g * HEAD : (g + 1) * HEAD]
            vx_ref[g, j * rows : (j + 1) * rows, HEAD:] = jnp.ones((rows, HEAD), vx_ref.dtype)
    docs = docs_ref[...]
    for turn in range(turns):
        here = turn * BLOCK
        first = count(docs < docs[:, here : here + 1]) // BLOCK
        q_copy(turn).wait()
        for n in range(1, turn + 2):

            @pl.when(turn - first + 1 == n)
            def _(turn=turn, n=n):
                width = n * BLOCK
                here = turn * BLOCK
                base = here + BLOCK - width
                q_docs = row_column(docs_ref[:, here : here + BLOCK])
                k_docs = docs_ref[:, base : base + width]
                ahead = lax.broadcasted_iota(jnp.int32, (BLOCK, width), 1) - lax.broadcasted_iota(
                    jnp.int32, (BLOCK, width), 0
                )
                keep = (jnp.concatenate([q_docs] * (width // HEAD), axis=1) == k_docs) & (ahead <= width - BLOCK)
                bias_ref[:, :width] = jnp.where(keep, 0.0, NEG)
                found = []
                for h in range(groups * share):
                    g = h // share
                    lanes = slice(h * HEAD, (h + 1) * HEAD)
                    k = k_ref[base : base + width, g * HEAD : (g + 1) * HEAD]
                    s = f32_dot(q_ref[turn, :, lanes], k, NT) * SCALE2 + bias_ref[:, :width]
                    top = jnp.max(s, axis=1, keepdims=True)
                    p = jnp.exp2(s - top).astype(jnp.bfloat16)
                    got = f32_dot(p, vx_ref[g, base : base + width, :], NN)
                    total = got[:, HEAD:]
                    o_ref[turn, :, lanes] = (got[:, :HEAD] / total).astype(o_ref.dtype)
                    found.append(eye_rows(top + jnp.log2(total)))
                l_ref[:, here : here + BLOCK] = jnp.concatenate(found, axis=0)

        o_copy(turn).start()
    for turn in range(turns):
        o_copy(turn).wait()


def own_part(queries, kv, docs):
    tok, width = queries.shape
    groups = kv.shape[2] // HEAD
    turns = tok // BLOCK
    return pl.pallas_call(
        own_kernel,
        in_specs=[IN_HBM, IN_VMEM, IN_VMEM],
        out_specs=(IN_HBM, IN_VMEM),
        out_shape=(
            jax.ShapeDtypeStruct((tok, width), jnp.bfloat16),
            jax.ShapeDtypeStruct((width // HEAD, tok), jnp.float32),
        ),
        scratch_shapes=[
            pltpu.VMEM((turns, BLOCK, width), jnp.bfloat16),
            pltpu.VMEM((turns, BLOCK, width), jnp.bfloat16),
            pltpu.VMEM((tok, groups * HEAD), jnp.bfloat16),
            pltpu.VMEM((groups, tok, 2 * HEAD), jnp.bfloat16),
            pltpu.VMEM((BLOCK, tok), jnp.float32),
            pltpu.SemaphoreType.DMA((turns,)),
            pltpu.SemaphoreType.DMA((turns,)),
        ],
        compiler_params=pltpu.CompilerParams(vmem_limit_bytes=VMEM_LIMIT),
        cost_estimate=pl.CostEstimate(
            flops=4 * tok * tok * width, bytes_accessed=4 * tok * width, transcendentals=tok * tok * width // HEAD // 2
        ),
    )(queries, kv, docs)


def rest_kernel(size, owner_ref, q_hbm, lown_ref, docs_ref, *refs):
    old_refs = refs[:size]
    done_hbm, o_hbm, send_ref, q_ref, o_ref, k_ref, vx_ref, got_ref, new_ref, l_ref, q_sem, d_sem, o_sem = refs[size:]
    del done_hbm
    turns = q_ref.shape[0]
    groups = vx_ref.shape[0]
    heads = q_ref.shape[2] // HEAD
    share = heads // groups
    rows = (old_refs[0].shape[0] - INFO) // 2
    tok = turns * BLOCK

    info = old_refs[0][2 * rows :, :HEAD].astype(jnp.float32)
    docs = docs_ref[...]
    same = info[0:1] == docs[:, :1].astype(jnp.float32)
    ahead = jnp.max(jnp.where(same, info[1:2] * CODE + info[2:3], 0.0)).astype(jnp.int32)
    behind = count(docs == docs[:, :1])
    steps = jnp.where(ahead > 0, (behind + BLOCK - 1) // BLOCK, 0)

    def q_copy(turn):
        return pltpu.make_async_copy(tile_of(q_hbm, turn), q_ref.at[turn], q_sem.at[turn])

    def d_copy(turn):
        return pltpu.make_async_copy(tile_of(o_hbm, turn), o_ref.at[turn], d_sem.at[turn])

    def o_copy(turn):
        return pltpu.make_async_copy(o_ref.at[turn], tile_of(o_hbm, turn), o_sem.at[turn])

    l_ref[...] = lown_ref[...]

    @pl.when(steps > 0)
    def _():
        for turn in range(turns):

            @pl.when(turn < steps)
            def _(turn=turn):
                q_copy(turn).start()
                d_copy(turn).start()

        here = lax.axis_index("head")
        for m in range(size):
            base = pl.multiple_of(lax.rem(here + size - m, size) * rows, rows)
            k_ref[pl.ds(base, rows), :] = old_refs[m][:rows]
            for g in range(groups):
                vx_ref[g, pl.ds(base, rows), :HEAD] = old_refs[m][rows : 2 * rows, g * HEAD : (g + 1) * HEAD]
                vx_ref[g, pl.ds(base, rows), HEAD:] = jnp.ones((rows, HEAD), vx_ref.dtype)

        def one(turn, _):
            q_copy(turn).wait()
            d_copy(turn).wait()
            for n in range(1, turns + 1):

                @pl.when((ahead + BLOCK - 1) // BLOCK == n)
                def _(n=n):
                    width = n * BLOCK
                    place = lax.broadcasted_iota(jnp.int32, (1, width), 1)
                    bias = jnp.where(place >= width - ahead, 0.0, NEG)
                    for h in range(heads):
                        g = h // share
                        k = k_ref[tok - width :, g * HEAD : (g + 1) * HEAD]
                        s = f32_dot(q_ref[turn, :, h * HEAD : (h + 1) * HEAD], k, NT) * SCALE2 + bias
                        top = jnp.max(s, axis=1, keepdims=True)
                        p = jnp.exp2(s - top).astype(jnp.bfloat16)
                        got = f32_dot(p, vx_ref[g, tok - width :, :], NN)
                        total = got[:, HEAD:]
                        got_ref[h] = got[:, :HEAD] / total
                        new_ref[h : h + 1, :] = eye_rows(top + jnp.log2(total))

            start = pl.multiple_of(turn * BLOCK, BLOCK)
            token = start + lax.broadcasted_iota(jnp.int32, (heads, BLOCK), 1)
            old = lown_ref[:, pl.ds(start, BLOCK)]
            new = jnp.where(token < behind, new_ref[...], NEG)
            most = jnp.maximum(new, old)
            both = most + jnp.log2(jnp.exp2(new - most) + jnp.exp2(old - most))
            l_ref[:, pl.ds(start, BLOCK)] = both
            part = jnp.exp2(new - both)
            for h in range(heads):
                lanes = slice(h * HEAD, (h + 1) * HEAD)
                before = o_ref[turn, :, lanes].astype(jnp.float32)
                mixed = before + row_column(part[h : h + 1]) * (got_ref[h] - before)
                o_ref[turn, :, lanes] = mixed.astype(o_ref.dtype)
            o_copy(turn).start()
            return 0

        lax.fori_loop(0, steps, one, 0)

    owners, _, piece = send_ref.shape
    for o in range(owners):
        found = jnp.zeros(send_ref.shape[1:], jnp.float32)
        for j in range(tok // piece):
            found = jnp.where(owner_ref[j] == o, l_ref[:, j * piece : (j + 1) * piece] * LN2, found)
        send_ref[o] = found

    for turn in range(turns):

        @pl.when(turn < steps)
        def _(turn=turn):
            o_copy(turn).wait()


def rest_part(owner, queries, lown, docs, old, done, owners, piece):
    tok, width = queries.shape
    size = len(old)
    heads = width // HEAD
    groups = old[0].shape[1] // HEAD
    turns = tok // BLOCK

    def kernel(*refs):
        rest_kernel(size, *refs)

    return pl.pallas_call(
        kernel,
        in_specs=[IN_SMEM, IN_HBM, IN_VMEM, IN_VMEM] + [IN_VMEM] * size + [IN_HBM],
        out_specs=(IN_HBM, IN_VMEM),
        out_shape=(
            jax.ShapeDtypeStruct((tok, width), jnp.bfloat16),
            jax.ShapeDtypeStruct((owners, heads, piece), jnp.float32),
        ),
        input_output_aliases={4 + size: 0},
        scratch_shapes=[
            pltpu.VMEM((turns, BLOCK, width), jnp.bfloat16),
            pltpu.VMEM((turns, BLOCK, width), jnp.bfloat16),
            pltpu.VMEM((tok, groups * HEAD), jnp.bfloat16),
            pltpu.VMEM((groups, tok, 2 * HEAD), jnp.bfloat16),
            pltpu.VMEM((heads, BLOCK, HEAD), jnp.float32),
            pltpu.VMEM((heads, BLOCK), jnp.float32),
            pltpu.VMEM((heads, tok), jnp.float32),
            pltpu.SemaphoreType.DMA((turns,)),
            pltpu.SemaphoreType.DMA((turns,)),
            pltpu.SemaphoreType.DMA((turns,)),
        ],
        compiler_params=pltpu.CompilerParams(vmem_limit_bytes=VMEM_LIMIT),
        cost_estimate=pl.CostEstimate(
            flops=tok * tok * width, bytes_accessed=4 * tok * width, transcendentals=tok * tok * heads // 4
        ),
    )(owner, queries, lown, docs, *old, done)


def spread_kernel(x_ref, o_ref):
    owners, _, piece = x_ref.shape
    for i in range(owners):
        o_ref[0, :, i * piece : (i + 1) * piece] = x_ref[i]


def spread(got):
    owners, heads, piece = got.shape
    return pl.pallas_call(
        spread_kernel,
        out_shape=jax.ShapeDtypeStruct((1, heads, owners * piece), got.dtype),
        cost_estimate=pl.CostEstimate(flops=0, bytes_accessed=8 * got.size, transcendentals=0),
    )(got)


def per_device(queries, keys, values, doc_ids, piece_owner):
    ctx_size, head_size = lax.axis_size("ctx"), lax.axis_size("head")
    tok, _ = queries.shape
    piece = 2 * tok // ctx_size
    docs = doc_ids.reshape(1, tok)

    own_send, *next_send = prep(keys, values, docs, head_size)
    kv = lax.all_to_all(own_send, "head", 0, 0, tiled=True)
    old = []
    for m in range(head_size):
        route = [
            (h * ctx_size + i, (h + m) % head_size * ctx_size + i + 1)
            for h in range(head_size)
            for i in range(ctx_size - 1)
        ]
        old.append(lax.ppermute(next_send[m], ("head", "ctx"), route))

    done, lown = own_part(queries, kv, docs)
    attended, send = rest_part(piece_owner, queries, lown, docs, old, done, ctx_size, piece)
    got = lax.all_to_all(send, "ctx", 0, 0, tiled=True)
    return attended, spread(got)


def solution(mesh):
    return jax.shard_map(
        per_device,
        mesh=mesh,
        in_specs=(
            P("ctx", "head"),
            P("ctx", "head", None),
            P("ctx", "head", None),
            P("ctx"),
            P("ctx"),
        ),
        out_specs=(P("ctx", "head"), P("ctx", "head", None)),
        check_vma=False,
    )
```

```python
import math

import jax
import jax.numpy as jnp
from jax import lax
from jax.experimental import pallas as pl
from jax.experimental.pallas import tpu as pltpu
from jax.sharding import PartitionSpec as P

HEAD = 128
BLOCK = 256
INFO = 16
CODE = 32
NEG = -1e30
FLOOR = 60.0
CEILING = 90.0
SCALE2 = HEAD ** (-0.5) * math.log2(math.e)
LN2 = math.log(2.0)
VMEM_LIMIT = 50 * 1024 * 1024
NT = (((1,), (1,)), ((), ()))
NN = (((1,), (0,)), ((), ()))
IN_VMEM = pl.BlockSpec(memory_space=pltpu.VMEM)
IN_SMEM = pl.BlockSpec(memory_space=pltpu.SMEM)
IN_HBM = pl.BlockSpec(memory_space=pltpu.HBM)


def f32_dot(a, b, dims):
    return lax.dot_general(a, b, dims, preferred_element_type=jnp.float32)


def eye_rows(column):
    eye = lax.broadcasted_iota(jnp.int32, (HEAD, HEAD), 0) == lax.broadcasted_iota(jnp.int32, (HEAD, HEAD), 1)
    parts = [
        jnp.sum(jnp.where(eye, column[i : i + HEAD], 0.0), axis=0, keepdims=True)
        for i in range(0, column.shape[0], HEAD)
    ]
    return jnp.concatenate(parts, axis=1)


def row_column(row):
    return jnp.broadcast_to(row, (HEAD, row.shape[1])).T


def count(flags):
    return jnp.sum(flags.astype(jnp.int32))


def tile_of(ref, turn):
    return ref.at[pl.ds(pl.multiple_of(turn * BLOCK, BLOCK), BLOCK), :]


def prep_kernel(size, k_ref, v_ref, docs_ref, own_ref, *next_refs):
    here = lax.axis_index("head")
    rows, cols = k_ref.shape[1], k_ref.shape[2] // size
    for j in range(size):
        own_ref[j, :rows] = k_ref[0, :, j * cols : (j + 1) * cols]
        own_ref[j, rows:] = v_ref[0, :, j * cols : (j + 1) * cols]
    docs = docs_ref[...]
    last = docs[:, docs.shape[1] - 1 :]
    run = jnp.sum(jnp.where(docs == last, 1.0, 0.0), axis=1, keepdims=True)
    high = jnp.floor(run * (1.0 / CODE))
    line = lax.broadcasted_iota(jnp.int32, (INFO, cols), 0)
    info = jnp.where(line == 0, last.astype(jnp.float32), jnp.where(line == 1, high, run - high * CODE))
    info = info.astype(k_ref.dtype)
    for m in range(size):
        start = pl.multiple_of(lax.rem(here + m, size) * cols, cols)
        next_refs[m][:rows] = k_ref[0, :, pl.ds(start, cols)]
        next_refs[m][rows : 2 * rows] = v_ref[0, :, pl.ds(start, cols)]
        next_refs[m][2 * rows :] = info


def prep(keys, values, docs, size):
    _, rows, width = keys.shape
    cols = width // size
    own = jax.ShapeDtypeStruct((size, 2 * rows, cols), keys.dtype)
    onward = jax.ShapeDtypeStruct((2 * rows + INFO, cols), keys.dtype)

    def kernel(*refs):
        prep_kernel(size, *refs)

    return pl.pallas_call(
        kernel,
        out_shape=(own,) + (onward,) * size,
        in_specs=[IN_VMEM] * 3,
        out_specs=(IN_VMEM,) * (size + 1),
        cost_estimate=pl.CostEstimate(flops=0, bytes_accessed=12 * keys.size, transcendentals=0),
    )(keys, values, docs)


def own_kernel(q_ref, kv_ref, docs_ref, o_ref, l_ref, k_ref, vx_ref, bias_ref, first_ref):
    turn = pl.program_id(1)
    parts, rows = kv_ref.shape[0], kv_ref.shape[1] // 2
    tok = parts * rows
    turns = tok // BLOCK
    share = q_ref.shape[1] // HEAD

    @pl.when(turn == 0)
    def _():
        for j in range(parts):
            k_ref[j * rows : (j + 1) * rows] = kv_ref[j, :rows]
            vx_ref[j * rows : (j + 1) * rows, :HEAD] = kv_ref[j, rows:]
            vx_ref[j * rows : (j + 1) * rows, HEAD:] = jnp.ones((rows, HEAD), vx_ref.dtype)

    @pl.when((turn == 0) & (pl.program_id(0) == 0))
    def _():
        docs = docs_ref[...]
        for t in range(turns):
            first_ref[t] = count(docs < docs[:, t * BLOCK : t * BLOCK + 1]) // BLOCK

    first = first_ref[turn]
    for n in range(1, turns + 1):

        @pl.when(turn - first + 1 == n)
        def _(n=n):
            width = n * BLOCK
            base = pl.multiple_of(first * BLOCK, BLOCK)
            here = pl.multiple_of(turn * BLOCK, BLOCK)
            q_docs = row_column(docs_ref[:, pl.ds(here, BLOCK)])
            k_docs = docs_ref[:, pl.ds(base, width)]
            ahead = lax.broadcasted_iota(jnp.int32, (BLOCK, width), 1) - lax.broadcasted_iota(
                jnp.int32, (BLOCK, width), 0
            )
            keep = (jnp.concatenate([q_docs] * (width // HEAD), axis=1) == k_docs) & (ahead <= width - BLOCK)
            bias_ref[:, :width] = jnp.where(keep, 0.0, NEG)
            k = k_ref[pl.ds(base, width), :]
            vx = vx_ref[pl.ds(base, width), :]
            for h in range(share):
                lanes = slice(h * HEAD, (h + 1) * HEAD)
                s = f32_dot(q_ref[:, lanes], k, NT) * SCALE2 + bias_ref[:, :width]
                got = f32_dot(jnp.exp2(s).astype(jnp.bfloat16), vx, NN)
                total = got[:, HEAD:]
                o_ref[:, lanes] = (got[:, :HEAD] / total).astype(o_ref.dtype)
                l_ref[h : h + 1, :] = eye_rows(jnp.log2(total))


def own_part(queries, kv, docs):
    tok, width = queries.shape
    parts, twice, cols = kv.shape
    groups = cols // HEAD
    turns = tok // BLOCK
    share = width // HEAD // groups
    return pl.pallas_call(
        own_kernel,
        grid=(groups, turns),
        in_specs=[
            pl.BlockSpec((BLOCK, share * HEAD), lambda g, t: (t, g)),
            pl.BlockSpec((parts, twice, HEAD), lambda g, t: (0, 0, g)),
            pl.BlockSpec((1, tok), lambda g, t: (0, 0)),
        ],
        out_specs=(
            pl.BlockSpec((BLOCK, share * HEAD), lambda g, t: (t, g)),
            pl.BlockSpec((share, BLOCK), lambda g, t: (g, t)),
        ),
        out_shape=(
            jax.ShapeDtypeStruct((tok, width), jnp.bfloat16),
            jax.ShapeDtypeStruct((width // HEAD, tok), jnp.float32),
        ),
        scratch_shapes=[
            pltpu.VMEM((tok, HEAD), jnp.bfloat16),
            pltpu.VMEM((tok, 2 * HEAD), jnp.bfloat16),
            pltpu.VMEM((BLOCK, tok), jnp.float32),
            pltpu.SMEM((turns,), jnp.int32),
        ],
        compiler_params=pltpu.CompilerParams(vmem_limit_bytes=VMEM_LIMIT),
        cost_estimate=pl.CostEstimate(
            flops=4 * tok * tok * width, bytes_accessed=4 * tok * width, transcendentals=tok * tok * width // HEAD // 2
        ),
    )(queries, kv, docs)


def beyond(logs):
    return jnp.logical_not((logs > -FLOOR) & (logs < CEILING))


def rest_kernel(size, owner_ref, q_hbm, lown_ref, docs_ref, kv_ref, *refs):
    old_refs = refs[:size]
    done_hbm, o_hbm, send_ref, q_ref, o_ref, k_ref, vx_ref, new_ref, l_ref, acc_ref, top_ref = refs[size : size + 11]
    q_sem, d_sem, o_sem = refs[size + 11 :]
    del done_hbm
    turns = q_ref.shape[0]
    groups = vx_ref.shape[0]
    heads = q_ref.shape[2] // HEAD
    share = heads // groups
    rows = (old_refs[0].shape[0] - INFO) // 2
    tok = turns * BLOCK

    info = old_refs[0][2 * rows :, :HEAD].astype(jnp.float32)
    docs = docs_ref[...]
    same = info[0:1] == docs[:, :1].astype(jnp.float32)
    ahead = jnp.max(jnp.where(same, info[1:2] * CODE + info[2:3], 0.0)).astype(jnp.int32)
    behind = count(docs == docs[:, :1])
    steps = jnp.where(ahead > 0, (behind + BLOCK - 1) // BLOCK, 0)

    def q_copy(turn):
        return pltpu.make_async_copy(tile_of(q_hbm, turn), q_ref.at[turn], q_sem.at[turn])

    def d_copy(turn):
        return pltpu.make_async_copy(tile_of(o_hbm, turn), o_ref.at[turn], d_sem.at[turn])

    def o_copy(turn):
        return pltpu.make_async_copy(o_ref.at[turn], tile_of(o_hbm, turn), o_sem.at[turn])

    for turn in range(turns):

        @pl.when(turn < steps)
        def _(turn=turn):
            q_copy(turn).start()
            d_copy(turn).start()

    new_ref[...] = jnp.zeros(new_ref.shape, jnp.float32)
    here = lax.axis_index("head")
    for m in range(size):
        base = pl.multiple_of(lax.rem(here + size - m, size) * rows, rows)
        for g in range(groups):
            lanes = slice(g * HEAD, (g + 1) * HEAD)
            k_ref[g, pl.ds(base, rows), :] = old_refs[m][:rows, lanes]
            vx_ref[g, pl.ds(base, rows), :HEAD] = old_refs[m][rows : 2 * rows, lanes]
            vx_ref[g, pl.ds(base, rows), HEAD:] = jnp.ones((rows, HEAD), vx_ref.dtype)

    def one(turn, _):
        q_copy(turn).wait()
        d_copy(turn).wait()
        start = pl.multiple_of(turn * BLOCK, BLOCK)
        inside = start + lax.broadcasted_iota(jnp.int32, (BLOCK, HEAD), 0) < behind
        for n in range(1, turns + 1):

            @pl.when((ahead + BLOCK - 1) // BLOCK == n)
            def _(n=n):
                width = n * BLOCK
                place = lax.broadcasted_iota(jnp.int32, (1, width), 1)
                bias = jnp.where(place >= width - ahead, 0.0, NEG)

                def one_group(g, _):
                    k = k_ref[g, tok - width :, :]
                    vx = vx_ref[g, tok - width :, :]
                    top_head = pl.multiple_of(g * share, share)
                    weights = jnp.exp2(lown_ref[pl.ds(top_head, share), pl.ds(start, BLOCK)])
                    found = []
                    for h in range(share):
                        lanes = pl.ds(pl.multiple_of((g * share + h) * HEAD, HEAD), HEAD)
                        s = f32_dot(q_ref[turn, :, lanes], k, NT) * SCALE2 + bias
                        got = f32_dot(jnp.exp2(s).astype(jnp.bfloat16), vx, NN)
                        total = jnp.where(inside, got[:, HEAD:], 0.0)
                        before = o_ref[turn, :, lanes].astype(jnp.float32)
                        weight = row_column(weights[h : h + 1])
                        mixed = (before * weight + got[:, :HEAD]) / (weight + total)
                        o_ref[turn, :, lanes] = jnp.where(inside, mixed, before).astype(o_ref.dtype)
                        found.append(eye_rows(total))
                    new_ref[pl.ds(top_head, share), pl.ds(start, BLOCK)] = jnp.concatenate(found, axis=0)
                    return 0

                lax.fori_loop(0, groups, one_group, 0)

        o_copy(turn).start()
        return 0

    lax.fori_loop(0, steps, one, 0)
    own = lown_ref[...]
    new = new_ref[...]
    l_ref[...] = jnp.log2(jnp.exp2(own) + new)
    token = lax.broadcasted_iota(jnp.int32, (heads, tok), 1)
    met = (token < behind) & (ahead > 0)
    bad = count(beyond(own) | (met & beyond(jnp.log2(new))))
    for turn in range(turns):

        @pl.when(turn < steps)
        def _(turn=turn):
            o_copy(turn).wait()

    @pl.when(bad > 0)
    def _():
        def every(turn, _):
            q_copy(turn).start()
            q_copy(turn).wait()
            start = pl.multiple_of(turn * BLOCK, BLOCK)
            q_docs = row_column(docs_ref[:, pl.ds(start, BLOCK)])
            q_docs = jnp.concatenate([q_docs] * (BLOCK // HEAD), axis=1)
            row = start + lax.broadcasted_iota(jnp.int32, (BLOCK, BLOCK), 0)
            column = lax.broadcasted_iota(jnp.int32, (BLOCK, BLOCK), 1)

            def one_head(h, _):
                g = h // share
                lanes = pl.ds(pl.multiple_of(h * HEAD, HEAD), HEAD)
                q = q_ref[turn, :, lanes]
                acc_ref[...] = jnp.zeros(acc_ref.shape, jnp.float32)
                top_ref[...] = jnp.full(top_ref.shape, NEG, jnp.float32)

                def add(keep, k, v):
                    s = jnp.where(keep, f32_dot(q, k, NT) * SCALE2, NEG)
                    before = top_ref[...]
                    top = jnp.maximum(before, jnp.max(s, axis=1, keepdims=True))
                    shift = jnp.exp2(before - top)
                    p = jnp.where(keep, jnp.exp2(s - jnp.concatenate([top] * (BLOCK // HEAD), axis=1)), 0.0)
                    p = p.astype(jnp.bfloat16)
                    ones = jnp.ones(v.shape, v.dtype)
                    acc_ref[:, :HEAD] = acc_ref[:, :HEAD] * shift + f32_dot(p, v, NN)
                    acc_ref[:, HEAD:] = acc_ref[:, HEAD:] * shift + f32_dot(p, ones, NN)
                    top_ref[...] = top

                def old_block(j, _):
                    at = pl.multiple_of(j * BLOCK, BLOCK)
                    keep = (j * BLOCK + column >= tok - ahead) & (row < behind)
                    add(keep, k_ref[g, pl.ds(at, BLOCK), :], vx_ref[g, pl.ds(at, BLOCK), :HEAD])
                    return 0

                def own_block(j, _):
                    at = pl.multiple_of(j * BLOCK, BLOCK)
                    keep = (q_docs == docs_ref[:, pl.ds(at, BLOCK)]) & (j * BLOCK + column <= row)
                    per = BLOCK // rows
                    group = pl.ds(pl.multiple_of(g * HEAD, HEAD), HEAD)
                    k = jnp.concatenate([kv_ref[j * per + i, :rows, group] for i in range(per)], axis=0)
                    v = jnp.concatenate([kv_ref[j * per + i, rows:, group] for i in range(per)], axis=0)
                    add(keep, k, v)
                    return 0

                lax.fori_loop(0, turns, old_block, 0)
                lax.fori_loop(0, turn + 1, own_block, 0)
                total = acc_ref[:, HEAD:]
                o_ref[turn, :, lanes] = (acc_ref[:, :HEAD] / total).astype(o_ref.dtype)
                l_ref[pl.ds(h, 1), pl.ds(start, BLOCK)] = eye_rows(top_ref[...] + jnp.log2(total))
                return 0

            lax.fori_loop(0, heads, one_head, 0)
            o_copy(turn).start()
            o_copy(turn).wait()
            return 0

        lax.fori_loop(0, turns, every, 0)

    owners, _, piece = send_ref.shape
    for o in range(owners):
        found = jnp.zeros(send_ref.shape[1:], jnp.float32)
        for j in range(tok // piece):
            found = jnp.where(owner_ref[j] == o, l_ref[:, j * piece : (j + 1) * piece] * LN2, found)
        send_ref[o] = found


def rest_part(owner, queries, lown, docs, kv, old, done, owners, piece):
    tok, width = queries.shape
    size = len(old)
    heads = width // HEAD
    groups = old[0].shape[1] // HEAD
    turns = tok // BLOCK

    def kernel(*refs):
        rest_kernel(size, *refs)

    return pl.pallas_call(
        kernel,
        in_specs=[IN_SMEM, IN_HBM, IN_VMEM, IN_VMEM, IN_VMEM] + [IN_VMEM] * size + [IN_HBM],
        out_specs=(IN_HBM, IN_VMEM),
        out_shape=(
            jax.ShapeDtypeStruct((tok, width), jnp.bfloat16),
            jax.ShapeDtypeStruct((owners, heads, piece), jnp.float32),
        ),
        input_output_aliases={5 + size: 0},
        scratch_shapes=[
            pltpu.VMEM((turns, BLOCK, width), jnp.bfloat16),
            pltpu.VMEM((turns, BLOCK, width), jnp.bfloat16),
            pltpu.VMEM((groups, tok, HEAD), jnp.bfloat16),
            pltpu.VMEM((groups, tok, 2 * HEAD), jnp.bfloat16),
            pltpu.VMEM((heads, tok), jnp.float32),
            pltpu.VMEM((heads, tok), jnp.float32),
            pltpu.VMEM((BLOCK, 2 * HEAD), jnp.float32),
            pltpu.VMEM((BLOCK, HEAD), jnp.float32),
            pltpu.SemaphoreType.DMA((turns,)),
            pltpu.SemaphoreType.DMA((turns,)),
            pltpu.SemaphoreType.DMA((turns,)),
        ],
        compiler_params=pltpu.CompilerParams(vmem_limit_bytes=VMEM_LIMIT),
        cost_estimate=pl.CostEstimate(
            flops=tok * tok * width, bytes_accessed=4 * tok * width, transcendentals=tok * tok * heads // 4
        ),
    )(owner, queries, lown, docs, kv, *old, done)


def spread_kernel(x_ref, o_ref):
    owners, _, piece = x_ref.shape
    for i in range(owners):
        o_ref[0, :, i * piece : (i + 1) * piece] = x_ref[i]


def spread(got):
    owners, heads, piece = got.shape
    return pl.pallas_call(
        spread_kernel,
        out_shape=jax.ShapeDtypeStruct((1, heads, owners * piece), got.dtype),
        cost_estimate=pl.CostEstimate(flops=0, bytes_accessed=8 * got.size, transcendentals=0),
    )(got)


def per_device(queries, keys, values, doc_ids, piece_owner):
    ctx_size, head_size = lax.axis_size("ctx"), lax.axis_size("head")
    tok, _ = queries.shape
    piece = 2 * tok // ctx_size
    docs = doc_ids.reshape(1, tok)

    own_send, *next_send = prep(keys, values, docs, head_size)
    kv = lax.all_to_all(own_send, "head", 0, 0, tiled=True)
    old = []
    for m in range(head_size):
        route = [
            (h * ctx_size + i, (h + m) % head_size * ctx_size + i + 1)
            for h in range(head_size)
            for i in range(ctx_size - 1)
        ]
        old.append(lax.ppermute(next_send[m], ("head", "ctx"), route))

    done, lown = own_part(queries, kv, docs)
    attended, send = rest_part(piece_owner, queries, lown, docs, kv, old, done, ctx_size, piece)
    got = lax.all_to_all(send, "ctx", 0, 0, tiled=True)
    return attended, spread(got)


def solution(mesh):
    return jax.shard_map(
        per_device,
        mesh=mesh,
        in_specs=(
            P("ctx", "head"),
            P("ctx", "head", None),
            P("ctx", "head", None),
            P("ctx"),
            P("ctx"),
        ),
        out_specs=(P("ctx", "head"), P("ctx", "head", None)),
        check_vma=False,
    )
```

```python
import itertools
import math

import jax
import jax.numpy as jnp
from jax import lax
from jax.experimental import pallas as pl
from jax.experimental.pallas import tpu as pltpu
from jax.sharding import PartitionSpec as P

HEAD = 128
BLOCK = 256
INFO = 16
CODE = 32
NEG = -1e30
FLOOR = 60.0
CEILING = 90.0
SCALE2 = HEAD ** (-0.5) * math.log2(math.e)
LN2 = math.log(2.0)
VMEM_LIMIT = 50 * 1024 * 1024
NT = (((1,), (1,)), ((), ()))
NN = (((1,), (0,)), ((), ()))
IN_VMEM = pl.BlockSpec(memory_space=pltpu.VMEM)
IN_SMEM = pl.BlockSpec(memory_space=pltpu.SMEM)
IN_HBM = pl.BlockSpec(memory_space=pltpu.HBM)


def f32_dot(a, b, dims):
    return lax.dot_general(a, b, dims, preferred_element_type=jnp.float32)


def eye_rows(column):
    eye = lax.broadcasted_iota(jnp.int32, (HEAD, HEAD), 0) == lax.broadcasted_iota(jnp.int32, (HEAD, HEAD), 1)
    parts = [
        jnp.sum(jnp.where(eye, column[i : i + HEAD], 0.0), axis=0, keepdims=True)
        for i in range(0, column.shape[0], HEAD)
    ]
    return jnp.concatenate(parts, axis=1)


def row_column(row):
    return jnp.broadcast_to(row, (HEAD, row.shape[1])).T


def count(flags):
    return jnp.sum(flags.astype(jnp.int32))


def tile_of(ref, turn):
    return ref.at[pl.ds(pl.multiple_of(turn * BLOCK, BLOCK), BLOCK), :]


def prep_kernel(size, k_ref, v_ref, docs_ref, own_ref, *next_refs):
    here = lax.axis_index("head")
    rows, cols = k_ref.shape[1], k_ref.shape[2] // size
    docs = docs_ref[...]
    last = docs[:, docs.shape[1] - 1 :]
    run = jnp.sum(jnp.where(docs == last, 1.0, 0.0), axis=1, keepdims=True)
    high = jnp.floor(run * (1.0 / CODE))
    line = lax.broadcasted_iota(jnp.int32, (INFO, cols), 0)
    info = jnp.where(line == 0, last.astype(jnp.float32), jnp.where(line == 1, high, run - high * CODE))
    info = info.astype(k_ref.dtype)
    ids = docs.astype(jnp.float32)
    table = jnp.zeros((INFO, cols), jnp.float32)
    for i in range(docs.shape[1] // cols):
        table = jnp.where(line == i, ids[:, i * cols : (i + 1) * cols], table)
    table = table.astype(k_ref.dtype)
    for j in range(size):
        own_ref[j, :rows] = k_ref[0, :, j * cols : (j + 1) * cols]
        own_ref[j, rows : 2 * rows] = v_ref[0, :, j * cols : (j + 1) * cols]
        own_ref[j, 2 * rows :] = table
    for m in range(size):
        start = pl.multiple_of(jnp.bitwise_xor(here, m) * cols, cols)
        next_refs[m][:rows] = k_ref[0, :, pl.ds(start, cols)]
        next_refs[m][rows : 2 * rows] = v_ref[0, :, pl.ds(start, cols)]
        next_refs[m][2 * rows :] = info


def prep(keys, values, docs, size):
    _, rows, width = keys.shape
    cols = width // size
    own = jax.ShapeDtypeStruct((size, 2 * rows + INFO, cols), keys.dtype)
    onward = jax.ShapeDtypeStruct((2 * rows + INFO, cols), keys.dtype)

    def kernel(*refs):
        prep_kernel(size, *refs)

    return pl.pallas_call(
        kernel,
        out_shape=(own,) + (onward,) * size,
        in_specs=[IN_VMEM] * 3,
        out_specs=(IN_VMEM,) * (size + 1),
        cost_estimate=pl.CostEstimate(flops=0, bytes_accessed=12 * keys.size, transcendentals=0),
    )(keys, values, docs)


def row_of_docs(kv_ref, tok):
    cols = kv_ref.shape[2]
    table = kv_ref[0, kv_ref.shape[1] - INFO :, :].astype(jnp.float32)
    return jnp.concatenate([table[i : i + 1] for i in range(tok // cols)], axis=1)


def own_kernel(q_ref, kv_ref, o_ref, l_ref, k_ref, vx_ref, bias_ref, docs_ref, first_ref):
    turn = pl.program_id(1)
    parts, rows = kv_ref.shape[0], (kv_ref.shape[1] - INFO) // 2
    group = pl.program_id(0)
    lanes = pl.ds(pl.multiple_of(group * HEAD, HEAD), HEAD)
    tok = parts * rows
    turns = tok // BLOCK
    share = q_ref.shape[1] // HEAD

    @pl.when(turn == 0)
    def _():
        for j in range(parts):
            k_ref[j * rows : (j + 1) * rows] = kv_ref[j, :rows, lanes]
            vx_ref[j * rows : (j + 1) * rows, :HEAD] = kv_ref[j, rows : 2 * rows, lanes]
            vx_ref[j * rows : (j + 1) * rows, HEAD:] = jnp.ones((rows, HEAD), vx_ref.dtype)

    @pl.when((turn == 0) & (group == 0))
    def _():
        docs = row_of_docs(kv_ref, tok)
        docs_ref[...] = docs
        for t in range(turns):
            first_ref[t] = count(docs < docs[:, t * BLOCK : t * BLOCK + 1]) // BLOCK

    first = first_ref[turn]
    for n in range(1, turns + 1):

        @pl.when(turn - first + 1 == n)
        def _(n=n):
            width = n * BLOCK
            base = pl.multiple_of(first * BLOCK, BLOCK)
            here = pl.multiple_of(turn * BLOCK, BLOCK)
            q_docs = row_column(docs_ref[:, pl.ds(here, BLOCK)])
            k_docs = docs_ref[:, pl.ds(base, width)]
            ahead = lax.broadcasted_iota(jnp.int32, (BLOCK, width), 1) - lax.broadcasted_iota(
                jnp.int32, (BLOCK, width), 0
            )
            keep = (jnp.concatenate([q_docs] * (width // HEAD), axis=1) == k_docs) & (ahead <= width - BLOCK)
            bias_ref[:, :width] = jnp.where(keep, 0.0, NEG)
            k = k_ref[pl.ds(base, width), :]
            vx = vx_ref[pl.ds(base, width), :]
            for h in range(share):
                lanes = slice(h * HEAD, (h + 1) * HEAD)
                s = f32_dot(q_ref[:, lanes], k, NT) * SCALE2 + bias_ref[:, :width]
                got = f32_dot(jnp.exp2(s).astype(jnp.bfloat16), vx, NN)
                total = got[:, HEAD:]
                o_ref[:, lanes] = (got[:, :HEAD] / total).astype(o_ref.dtype)
                l_ref[h : h + 1, :] = eye_rows(jnp.log2(total))


def own_part(queries, kv):
    tok, width = queries.shape
    parts, longer, cols = kv.shape
    groups = cols // HEAD
    turns = tok // BLOCK
    share = width // HEAD // groups
    return pl.pallas_call(
        own_kernel,
        grid=(groups, turns),
        in_specs=[
            pl.BlockSpec((BLOCK, share * HEAD), lambda g, t: (t, g)),
            pl.BlockSpec((parts, longer, cols), lambda g, t: (0, 0, 0)),
        ],
        out_specs=(
            pl.BlockSpec((BLOCK, share * HEAD), lambda g, t: (t, g)),
            pl.BlockSpec((share, BLOCK), lambda g, t: (g, t)),
        ),
        out_shape=(
            jax.ShapeDtypeStruct((tok, width), jnp.bfloat16),
            jax.ShapeDtypeStruct((width // HEAD, tok), jnp.float32),
        ),
        scratch_shapes=[
            pltpu.VMEM((tok, HEAD), jnp.bfloat16),
            pltpu.VMEM((tok, 2 * HEAD), jnp.bfloat16),
            pltpu.VMEM((BLOCK, tok), jnp.float32),
            pltpu.VMEM((1, tok), jnp.float32),
            pltpu.SMEM((turns,), jnp.int32),
        ],
        compiler_params=pltpu.CompilerParams(vmem_limit_bytes=VMEM_LIMIT),
        cost_estimate=pl.CostEstimate(
            flops=4 * tok * tok * width, bytes_accessed=4 * tok * width, transcendentals=tok * tok * width // HEAD // 2
        ),
    )(queries, kv)


def beyond(logs):
    return jnp.logical_not((logs > -FLOOR) & (logs < CEILING))


def rest_kernel(size, owner_ref, q_hbm, lown_ref, kv_ref, *refs):
    old_refs = refs[:size]
    done_hbm, o_hbm, send_ref, q_ref, o_ref, k_ref, vx_ref, new_ref, l_ref, acc_ref, top_ref = refs[size : size + 11]
    docs_ref, q_sem, d_sem, o_sem = refs[size + 11 :]
    del done_hbm
    turns = q_ref.shape[0]
    groups = vx_ref.shape[0]
    heads = q_ref.shape[2] // HEAD
    share = heads // groups
    rows = (old_refs[0].shape[0] - INFO) // 2
    tok = turns * BLOCK

    info = old_refs[0][2 * rows :, :HEAD].astype(jnp.float32)
    docs = row_of_docs(kv_ref, tok)
    same = info[0:1] == docs[:, :1]
    ahead = jnp.max(jnp.where(same, info[1:2] * CODE + info[2:3], 0.0)).astype(jnp.int32)
    behind = count(docs == docs[:, :1])
    steps = jnp.where(ahead > 0, (behind + BLOCK - 1) // BLOCK, 0)

    def q_copy(turn):
        return pltpu.make_async_copy(tile_of(q_hbm, turn), q_ref.at[turn], q_sem.at[turn])

    def d_copy(turn):
        return pltpu.make_async_copy(tile_of(o_hbm, turn), o_ref.at[turn], d_sem.at[turn])

    def o_copy(turn):
        return pltpu.make_async_copy(o_ref.at[turn], tile_of(o_hbm, turn), o_sem.at[turn])

    for turn in range(turns):

        @pl.when(turn < steps)
        def _(turn=turn):
            q_copy(turn).start()
            d_copy(turn).start()

    new_ref[...] = jnp.zeros(new_ref.shape, jnp.float32)
    here = lax.axis_index("head")
    for m in range(size):
        base = pl.multiple_of(jnp.bitwise_xor(here, m) * rows, rows)
        for g in range(groups):
            lanes = slice(g * HEAD, (g + 1) * HEAD)
            k_ref[g, pl.ds(base, rows), :] = old_refs[m][:rows, lanes]
            vx_ref[g, pl.ds(base, rows), :HEAD] = old_refs[m][rows : 2 * rows, lanes]
            vx_ref[g, pl.ds(base, rows), HEAD:] = jnp.ones((rows, HEAD), vx_ref.dtype)

    def one(turn, _):
        q_copy(turn).wait()
        d_copy(turn).wait()
        start = pl.multiple_of(turn * BLOCK, BLOCK)
        short = behind - start <= BLOCK // 2
        for n, tall in itertools.product(range(1, turns + 1), (BLOCK // 2, BLOCK)):

            @pl.when(((ahead + BLOCK - 1) // BLOCK == n) & (short == (tall < BLOCK)))
            def _(n=n, tall=tall):
                width = n * BLOCK
                inside = start + lax.broadcasted_iota(jnp.int32, (tall, HEAD), 0) < behind
                place = lax.broadcasted_iota(jnp.int32, (1, width), 1)
                bias = jnp.where(place >= width - ahead, 0.0, NEG)

                def one_group(g, _):
                    k = k_ref[g, tok - width :, :]
                    vx = vx_ref[g, tok - width :, :]
                    top_head = pl.multiple_of(g * share, share)
                    weights = jnp.exp2(lown_ref[pl.ds(top_head, share), pl.ds(start, tall)])
                    found = []
                    for h in range(share):
                        lanes = pl.ds(pl.multiple_of((g * share + h) * HEAD, HEAD), HEAD)
                        s = f32_dot(q_ref[turn, :tall, lanes], k, NT) * SCALE2 + bias
                        got = f32_dot(jnp.exp2(s).astype(jnp.bfloat16), vx, NN)
                        total = jnp.where(inside, got[:, HEAD:], 0.0)
                        before = o_ref[turn, :tall, lanes].astype(jnp.float32)
                        weight = row_column(weights[h : h + 1])
                        mixed = (before * weight + got[:, :HEAD]) / (weight + total)
                        o_ref[turn, :tall, lanes] = jnp.where(inside, mixed, before).astype(o_ref.dtype)
                        found.append(eye_rows(total))
                    new_ref[pl.ds(top_head, share), pl.ds(start, tall)] = jnp.concatenate(found, axis=0)
                    return 0

                lax.fori_loop(0, groups, one_group, 0)

        o_copy(turn).start()
        return 0

    lax.fori_loop(0, steps, one, 0)
    own = lown_ref[...]
    new = new_ref[...]
    l_ref[...] = jnp.log2(jnp.exp2(own) + new)
    token = lax.broadcasted_iota(jnp.int32, (heads, tok), 1)
    met = (token < behind) & (ahead > 0)
    bad = count(beyond(own) | (met & beyond(jnp.log2(new))))
    for turn in range(turns):

        @pl.when(turn < steps)
        def _(turn=turn):
            o_copy(turn).wait()

    @pl.when(bad > 0)
    def _():
        docs_ref[...] = docs

        def every(turn, _):
            q_copy(turn).start()
            q_copy(turn).wait()
            start = pl.multiple_of(turn * BLOCK, BLOCK)
            q_docs = row_column(docs_ref[:, pl.ds(start, BLOCK)])
            q_docs = jnp.concatenate([q_docs] * (BLOCK // HEAD), axis=1)
            row = start + lax.broadcasted_iota(jnp.int32, (BLOCK, BLOCK), 0)
            column = lax.broadcasted_iota(jnp.int32, (BLOCK, BLOCK), 1)

            def one_head(h, _):
                g = h // share
                lanes = pl.ds(pl.multiple_of(h * HEAD, HEAD), HEAD)
                q = q_ref[turn, :, lanes]
                acc_ref[...] = jnp.zeros(acc_ref.shape, jnp.float32)
                top_ref[...] = jnp.full(top_ref.shape, NEG, jnp.float32)

                def add(keep, k, v):
                    s = jnp.where(keep, f32_dot(q, k, NT) * SCALE2, NEG)
                    before = top_ref[...]
                    top = jnp.maximum(before, jnp.max(s, axis=1, keepdims=True))
                    shift = jnp.exp2(before - top)
                    p = jnp.where(keep, jnp.exp2(s - jnp.concatenate([top] * (BLOCK // HEAD), axis=1)), 0.0)
                    p = p.astype(jnp.bfloat16)
                    ones = jnp.ones(v.shape, v.dtype)
                    acc_ref[:, :HEAD] = acc_ref[:, :HEAD] * shift + f32_dot(p, v, NN)
                    acc_ref[:, HEAD:] = acc_ref[:, HEAD:] * shift + f32_dot(p, ones, NN)
                    top_ref[...] = top

                def old_block(j, _):
                    at = pl.multiple_of(j * BLOCK, BLOCK)
                    keep = (j * BLOCK + column >= tok - ahead) & (row < behind)
                    add(keep, k_ref[g, pl.ds(at, BLOCK), :], vx_ref[g, pl.ds(at, BLOCK), :HEAD])
                    return 0

                def own_block(j, _):
                    at = pl.multiple_of(j * BLOCK, BLOCK)
                    keep = (q_docs == docs_ref[:, pl.ds(at, BLOCK)]) & (j * BLOCK + column <= row)
                    per = BLOCK // rows
                    group = pl.ds(pl.multiple_of(g * HEAD, HEAD), HEAD)
                    k = jnp.concatenate([kv_ref[j * per + i, :rows, group] for i in range(per)], axis=0)
                    v = jnp.concatenate([kv_ref[j * per + i, rows : 2 * rows, group] for i in range(per)], axis=0)
                    add(keep, k, v)
                    return 0

                lax.fori_loop(0, turns, old_block, 0)
                lax.fori_loop(0, turn + 1, own_block, 0)
                total = acc_ref[:, HEAD:]
                o_ref[turn, :, lanes] = (acc_ref[:, :HEAD] / total).astype(o_ref.dtype)
                l_ref[pl.ds(h, 1), pl.ds(start, BLOCK)] = eye_rows(top_ref[...] + jnp.log2(total))
                return 0

            lax.fori_loop(0, heads, one_head, 0)
            o_copy(turn).start()
            o_copy(turn).wait()
            return 0

        lax.fori_loop(0, turns, every, 0)

    owners, _, piece = send_ref.shape
    for o in range(owners):
        found = jnp.zeros(send_ref.shape[1:], jnp.float32)
        for j in range(tok // piece):
            found = jnp.where(owner_ref[j] == o, l_ref[:, j * piece : (j + 1) * piece] * LN2, found)
        send_ref[o] = found


def rest_part(owner, queries, lown, kv, old, done, owners, piece):
    tok, width = queries.shape
    size = len(old)
    heads = width // HEAD
    groups = old[0].shape[1] // HEAD
    turns = tok // BLOCK

    def kernel(*refs):
        rest_kernel(size, *refs)

    return pl.pallas_call(
        kernel,
        in_specs=[IN_SMEM, IN_HBM, IN_VMEM, IN_VMEM] + [IN_VMEM] * size + [IN_HBM],
        out_specs=(IN_HBM, IN_VMEM),
        out_shape=(
            jax.ShapeDtypeStruct((tok, width), jnp.bfloat16),
            jax.ShapeDtypeStruct((owners, heads, piece), jnp.float32),
        ),
        input_output_aliases={4 + size: 0},
        scratch_shapes=[
            pltpu.VMEM((turns, BLOCK, width), jnp.bfloat16),
            pltpu.VMEM((turns, BLOCK, width), jnp.bfloat16),
            pltpu.VMEM((groups, tok, HEAD), jnp.bfloat16),
            pltpu.VMEM((groups, tok, 2 * HEAD), jnp.bfloat16),
            pltpu.VMEM((heads, tok), jnp.float32),
            pltpu.VMEM((heads, tok), jnp.float32),
            pltpu.VMEM((BLOCK, 2 * HEAD), jnp.float32),
            pltpu.VMEM((BLOCK, HEAD), jnp.float32),
            pltpu.VMEM((1, tok), jnp.float32),
            pltpu.SemaphoreType.DMA((turns,)),
            pltpu.SemaphoreType.DMA((turns,)),
            pltpu.SemaphoreType.DMA((turns,)),
        ],
        compiler_params=pltpu.CompilerParams(vmem_limit_bytes=VMEM_LIMIT),
        cost_estimate=pl.CostEstimate(
            flops=tok * tok * width, bytes_accessed=4 * tok * width, transcendentals=tok * tok * heads // 4
        ),
    )(owner, queries, lown, kv, *old, done)


def spread_kernel(x_ref, o_ref):
    owners, _, piece = x_ref.shape
    for i in range(owners):
        o_ref[0, :, i * piece : (i + 1) * piece] = x_ref[i]


def spread(got):
    owners, heads, piece = got.shape
    return pl.pallas_call(
        spread_kernel,
        out_shape=jax.ShapeDtypeStruct((1, heads, owners * piece), got.dtype),
        cost_estimate=pl.CostEstimate(flops=0, bytes_accessed=8 * got.size, transcendentals=0),
    )(got)


def per_device(queries, keys, values, doc_ids, piece_owner):
    ctx_size, head_size = lax.axis_size("ctx"), lax.axis_size("head")
    tok, _ = queries.shape
    piece = 2 * tok // ctx_size

    own_send, *next_send = prep(keys, values, doc_ids.reshape(1, tok), head_size)
    kv = lax.all_to_all(own_send, "head", 0, 0, tiled=True)
    old = []
    for m in range(head_size):
        route = [
            (h * ctx_size + i, (h ^ m) * ctx_size + i + 1)
            for h in range(head_size)
            for i in range(ctx_size - 1)
        ]
        old.append(lax.ppermute(next_send[m], ("head", "ctx"), route))

    done, lown = own_part(queries, kv)
    attended, send = rest_part(piece_owner, queries, lown, kv, old, done, ctx_size, piece)
    got = lax.all_to_all(send, "ctx", 0, 0, tiled=True)
    return attended, spread(got)


def solution(mesh):
    return jax.shard_map(
        per_device,
        mesh=mesh,
        in_specs=(
            P("ctx", "head"),
            P("ctx", "head", None),
            P("ctx", "head", None),
            P("ctx"),
            P("ctx"),
        ),
        out_specs=(P("ctx", "head"), P("ctx", "head", None)),
        check_vma=False,
    )
```

```python
import itertools
import math

import jax
import jax.numpy as jnp
from jax import lax
from jax.experimental import pallas as pl
from jax.experimental.pallas import tpu as pltpu
from jax.sharding import PartitionSpec as P

HEAD = 128
BLOCK = 256
INFO = 16
CODE = 32
NEG = -1e30
FLOOR = 60.0
CEILING = 90.0
SCALE2 = HEAD ** (-0.5) * math.log2(math.e)
LN2 = math.log(2.0)
VMEM_LIMIT = 50 * 1024 * 1024
NT = (((1,), (1,)), ((), ()))
NN = (((1,), (0,)), ((), ()))
IN_VMEM = pl.BlockSpec(memory_space=pltpu.VMEM)
IN_SMEM = pl.BlockSpec(memory_space=pltpu.SMEM)
IN_HBM = pl.BlockSpec(memory_space=pltpu.HBM)


def f32_dot(a, b, dims):
    return lax.dot_general(a, b, dims, preferred_element_type=jnp.float32)


def eye_rows(column):
    eye = lax.broadcasted_iota(jnp.int32, (HEAD, HEAD), 0) == lax.broadcasted_iota(jnp.int32, (HEAD, HEAD), 1)
    parts = [
        jnp.sum(jnp.where(eye, column[i : i + HEAD], 0.0), axis=0, keepdims=True)
        for i in range(0, column.shape[0], HEAD)
    ]
    return jnp.concatenate(parts, axis=1)


def row_column(row):
    return jnp.broadcast_to(row, (HEAD, row.shape[1])).T


def count(flags):
    return jnp.sum(flags.astype(jnp.int32))


def tile_of(ref, turn):
    return ref.at[pl.ds(pl.multiple_of(turn * BLOCK, BLOCK), BLOCK), :]


def prep_kernel(size, k_ref, v_ref, docs_ref, own_ref, *next_refs):
    here = lax.axis_index("head")
    rows, cols = k_ref.shape[1], k_ref.shape[2] // size
    docs = docs_ref[...]
    last = docs[:, docs.shape[1] - 1 :]
    run = jnp.sum(jnp.where(docs == last, 1.0, 0.0), axis=1, keepdims=True)
    high = jnp.floor(run * (1.0 / CODE))
    line = lax.broadcasted_iota(jnp.int32, (INFO, cols), 0)
    info = jnp.where(line == 0, last.astype(jnp.float32), jnp.where(line == 1, high, run - high * CODE))
    info = info.astype(k_ref.dtype)
    ids = docs.astype(jnp.float32)
    table = jnp.zeros((INFO, cols), jnp.float32)
    for i in range(docs.shape[1] // cols):
        table = jnp.where(line == i, ids[:, i * cols : (i + 1) * cols], table)
    table = table.astype(k_ref.dtype)
    for j in range(size):
        own_ref[j, :rows] = k_ref[0, :, j * cols : (j + 1) * cols]
        own_ref[j, rows : 2 * rows] = v_ref[0, :, j * cols : (j + 1) * cols]
        own_ref[j, 2 * rows :] = table
    for m in range(size):
        start = pl.multiple_of(jnp.bitwise_xor(here, m) * cols, cols)
        next_refs[m][:rows] = k_ref[0, :, pl.ds(start, cols)]
        next_refs[m][rows : 2 * rows] = v_ref[0, :, pl.ds(start, cols)]
        next_refs[m][2 * rows :] = info


def prep(keys, values, docs, size):
    _, rows, width = keys.shape
    cols = width // size
    own = jax.ShapeDtypeStruct((size, 2 * rows + INFO, cols), keys.dtype)
    onward = jax.ShapeDtypeStruct((2 * rows + INFO, cols), keys.dtype)

    def kernel(*refs):
        prep_kernel(size, *refs)

    return pl.pallas_call(
        kernel,
        out_shape=(own,) + (onward,) * size,
        in_specs=[IN_VMEM] * 3,
        out_specs=(IN_VMEM,) * (size + 1),
        cost_estimate=pl.CostEstimate(flops=0, bytes_accessed=12 * keys.size, transcendentals=0),
    )(keys, values, docs)


def row_of_docs(kv_ref, tok):
    cols = kv_ref.shape[2]
    table = kv_ref[0, kv_ref.shape[1] - INFO :, :].astype(jnp.float32)
    return jnp.concatenate([table[i : i + 1] for i in range(tok // cols)], axis=1)


def own_kernel(q_ref, kv_ref, o_ref, l_ref, k_ref, vx_ref, bias_ref, docs_ref, first_ref):
    turn = pl.program_id(0)
    parts, rows = kv_ref.shape[0], (kv_ref.shape[1] - INFO) // 2
    groups = vx_ref.shape[0]
    tok = parts * rows
    turns = tok // BLOCK
    share = q_ref.shape[1] // HEAD // groups

    @pl.when(turn == 0)
    def _():
        docs = row_of_docs(kv_ref, tok)
        docs_ref[...] = docs
        for t in range(turns):
            first_ref[t] = count(docs < docs[:, t * BLOCK : t * BLOCK + 1]) // BLOCK
        for j in range(parts):
            span = slice(j * rows, (j + 1) * rows)
            k_ref[span] = kv_ref[j, :rows]
            for g in range(groups):
                vx_ref[g, span, :HEAD] = kv_ref[j, rows : 2 * rows, g * HEAD : (g + 1) * HEAD]
                vx_ref[g, span, HEAD:] = jnp.ones((rows, HEAD), vx_ref.dtype)

    first = first_ref[turn]
    for n in range(1, turns + 1):

        @pl.when(turn - first + 1 == n)
        def _(n=n):
            width = n * BLOCK
            base = pl.multiple_of(first * BLOCK, BLOCK)
            here = pl.multiple_of(turn * BLOCK, BLOCK)
            q_docs = row_column(docs_ref[:, pl.ds(here, BLOCK)])
            k_docs = docs_ref[:, pl.ds(base, width)]
            ahead = lax.broadcasted_iota(jnp.int32, (BLOCK, width), 1) - lax.broadcasted_iota(
                jnp.int32, (BLOCK, width), 0
            )
            keep = (jnp.concatenate([q_docs] * (width // HEAD), axis=1) == k_docs) & (ahead <= width - BLOCK)
            bias_ref[:, :width] = jnp.where(keep, 0.0, NEG)
            for h in range(groups * share):
                g = h // share
                lanes = slice(h * HEAD, (h + 1) * HEAD)
                k = k_ref[pl.ds(base, width), g * HEAD : (g + 1) * HEAD]
                s = f32_dot(q_ref[:, lanes], k, NT) * SCALE2 + bias_ref[:, :width]
                got = f32_dot(jnp.exp2(s).astype(jnp.bfloat16), vx_ref[g, pl.ds(base, width), :], NN)
                total = got[:, HEAD:]
                o_ref[:, lanes] = (got[:, :HEAD] / total).astype(o_ref.dtype)
                l_ref[h : h + 1, :] = eye_rows(jnp.log2(total))


def own_part(queries, kv):
    tok, width = queries.shape
    groups = kv.shape[2] // HEAD
    return pl.pallas_call(
        own_kernel,
        grid=(tok // BLOCK,),
        in_specs=[
            pl.BlockSpec((BLOCK, width), lambda t: (t, 0)),
            pl.BlockSpec(kv.shape, lambda t: (0, 0, 0)),
        ],
        out_specs=(
            pl.BlockSpec((BLOCK, width), lambda t: (t, 0)),
            pl.BlockSpec((width // HEAD, BLOCK), lambda t: (0, t)),
        ),
        out_shape=(
            jax.ShapeDtypeStruct((tok, width), jnp.bfloat16),
            jax.ShapeDtypeStruct((width // HEAD, tok), jnp.float32),
        ),
        scratch_shapes=[
            pltpu.VMEM((tok, groups * HEAD), jnp.bfloat16),
            pltpu.VMEM((groups, tok, 2 * HEAD), jnp.bfloat16),
            pltpu.VMEM((BLOCK, tok), jnp.float32),
            pltpu.VMEM((1, tok), jnp.float32),
            pltpu.SMEM((tok // BLOCK,), jnp.int32),
        ],
        compiler_params=pltpu.CompilerParams(vmem_limit_bytes=VMEM_LIMIT),
        cost_estimate=pl.CostEstimate(
            flops=4 * tok * tok * width, bytes_accessed=4 * tok * width, transcendentals=tok * tok * width // HEAD // 2
        ),
    )(queries, kv)


def beyond(logs):
    return jnp.logical_not((logs > -FLOOR) & (logs < CEILING))


def rest_kernel(size, owner_ref, q_hbm, lown_ref, kv_ref, *refs):
    old_refs = refs[:size]
    done_hbm, o_hbm, send_ref, q_ref, o_ref, k_ref, vx_ref, new_ref, l_ref, acc_ref, top_ref = refs[size : size + 11]
    docs_ref, q_sem, d_sem, o_sem = refs[size + 11 :]
    del done_hbm
    turns = q_ref.shape[0]
    groups = vx_ref.shape[0]
    heads = q_ref.shape[2] // HEAD
    share = heads // groups
    rows = (old_refs[0].shape[0] - INFO) // 2
    tok = turns * BLOCK

    def q_copy(turn):
        return pltpu.make_async_copy(tile_of(q_hbm, turn), q_ref.at[turn], q_sem.at[turn])

    def d_copy(turn):
        return pltpu.make_async_copy(tile_of(o_hbm, turn), o_ref.at[turn], d_sem.at[turn])

    def o_copy(turn):
        return pltpu.make_async_copy(o_ref.at[turn], tile_of(o_hbm, turn), o_sem.at[turn])

    q_copy(0).start()
    d_copy(0).start()
    info = old_refs[0][2 * rows :, :HEAD].astype(jnp.float32)
    docs = row_of_docs(kv_ref, tok)
    same = info[0:1] == docs[:, :1]
    ahead = jnp.max(jnp.where(same, info[1:2] * CODE + info[2:3], 0.0)).astype(jnp.int32)
    behind = count(docs == docs[:, :1])
    steps = jnp.where(ahead > 0, (behind + BLOCK - 1) // BLOCK, 0)

    for turn in range(1, turns):

        @pl.when(turn < steps)
        def _(turn=turn):
            q_copy(turn).start()
            d_copy(turn).start()

    new_ref[...] = jnp.zeros(new_ref.shape, jnp.float32)
    here = lax.axis_index("head")
    for m in range(size):
        base = pl.multiple_of(jnp.bitwise_xor(here, m) * rows, rows)
        for g in range(groups):
            lanes = slice(g * HEAD, (g + 1) * HEAD)
            k_ref[g, pl.ds(base, rows), :] = old_refs[m][:rows, lanes]
            vx_ref[g, pl.ds(base, rows), :HEAD] = old_refs[m][rows : 2 * rows, lanes]
            vx_ref[g, pl.ds(base, rows), HEAD:] = jnp.ones((rows, HEAD), vx_ref.dtype)

    def one(turn, _):
        q_copy(turn).wait()
        d_copy(turn).wait()
        start = pl.multiple_of(turn * BLOCK, BLOCK)
        short = behind - start <= BLOCK // 2
        for n, tall in itertools.product(range(1, turns + 1), (BLOCK // 2, BLOCK)):

            @pl.when(((ahead + BLOCK - 1) // BLOCK == n) & (short == (tall < BLOCK)))
            def _(n=n, tall=tall):
                width = n * BLOCK
                inside = start + lax.broadcasted_iota(jnp.int32, (tall, HEAD), 0) < behind
                place = lax.broadcasted_iota(jnp.int32, (1, width), 1)
                bias = jnp.where(place >= width - ahead, 0.0, NEG)

                def one_group(g, _):
                    k = k_ref[g, tok - width :, :]
                    vx = vx_ref[g, tok - width :, :]
                    top_head = pl.multiple_of(g * share, share)
                    weights = jnp.exp2(lown_ref[pl.ds(top_head, share), pl.ds(start, tall)])
                    found = []
                    for h in range(share):
                        lanes = pl.ds(pl.multiple_of((g * share + h) * HEAD, HEAD), HEAD)
                        s = f32_dot(q_ref[turn, :tall, lanes], k, NT) * SCALE2 + bias
                        got = f32_dot(jnp.exp2(s).astype(jnp.bfloat16), vx, NN)
                        total = jnp.where(inside, got[:, HEAD:], 0.0)
                        before = o_ref[turn, :tall, lanes].astype(jnp.float32)
                        weight = row_column(weights[h : h + 1])
                        mixed = (before * weight + got[:, :HEAD]) / (weight + total)
                        o_ref[turn, :tall, lanes] = jnp.where(inside, mixed, before).astype(o_ref.dtype)
                        found.append(eye_rows(total))
                    new_ref[pl.ds(top_head, share), pl.ds(start, tall)] = jnp.concatenate(found, axis=0)
                    return 0

                lax.fori_loop(0, groups, one_group, 0)

        o_copy(turn).start()
        return 0

    lax.fori_loop(0, steps, one, 0)

    @pl.when(steps == 0)
    def _():
        q_copy(0).wait()
        d_copy(0).wait()

    own = lown_ref[...]
    new = new_ref[...]
    l_ref[...] = jnp.log2(jnp.exp2(own) + new)
    token = lax.broadcasted_iota(jnp.int32, (heads, tok), 1)
    met = (token < behind) & (ahead > 0)
    bad = count(beyond(own) | (met & beyond(jnp.log2(new))))
    for turn in range(turns):

        @pl.when(turn < steps)
        def _(turn=turn):
            o_copy(turn).wait()

    @pl.when(bad > 0)
    def _():
        docs_ref[...] = docs

        def every(turn, _):
            q_copy(turn).start()
            q_copy(turn).wait()
            start = pl.multiple_of(turn * BLOCK, BLOCK)
            q_docs = row_column(docs_ref[:, pl.ds(start, BLOCK)])
            q_docs = jnp.concatenate([q_docs] * (BLOCK // HEAD), axis=1)
            row = start + lax.broadcasted_iota(jnp.int32, (BLOCK, BLOCK), 0)
            column = lax.broadcasted_iota(jnp.int32, (BLOCK, BLOCK), 1)

            def one_head(h, _):
                g = h // share
                lanes = pl.ds(pl.multiple_of(h * HEAD, HEAD), HEAD)
                q = q_ref[turn, :, lanes]
                acc_ref[...] = jnp.zeros(acc_ref.shape, jnp.float32)
                top_ref[...] = jnp.full(top_ref.shape, NEG, jnp.float32)

                def add(keep, k, v):
                    s = jnp.where(keep, f32_dot(q, k, NT) * SCALE2, NEG)
                    before = top_ref[...]
                    top = jnp.maximum(before, jnp.max(s, axis=1, keepdims=True))
                    shift = jnp.exp2(before - top)
                    p = jnp.where(keep, jnp.exp2(s - jnp.concatenate([top] * (BLOCK // HEAD), axis=1)), 0.0)
                    p = p.astype(jnp.bfloat16)
                    ones = jnp.ones(v.shape, v.dtype)
                    acc_ref[:, :HEAD] = acc_ref[:, :HEAD] * shift + f32_dot(p, v, NN)
                    acc_ref[:, HEAD:] = acc_ref[:, HEAD:] * shift + f32_dot(p, ones, NN)
                    top_ref[...] = top

                def old_block(j, _):
                    at = pl.multiple_of(j * BLOCK, BLOCK)
                    keep = (j * BLOCK + column >= tok - ahead) & (row < behind)
                    add(keep, k_ref[g, pl.ds(at, BLOCK), :], vx_ref[g, pl.ds(at, BLOCK), :HEAD])
                    return 0

                def own_block(j, _):
                    at = pl.multiple_of(j * BLOCK, BLOCK)
                    keep = (q_docs == docs_ref[:, pl.ds(at, BLOCK)]) & (j * BLOCK + column <= row)
                    per = BLOCK // rows
                    group = pl.ds(pl.multiple_of(g * HEAD, HEAD), HEAD)
                    k = jnp.concatenate([kv_ref[j * per + i, :rows, group] for i in range(per)], axis=0)
                    v = jnp.concatenate([kv_ref[j * per + i, rows : 2 * rows, group] for i in range(per)], axis=0)
                    add(keep, k, v)
                    return 0

                lax.fori_loop(0, turns, old_block, 0)
                lax.fori_loop(0, turn + 1, own_block, 0)
                total = acc_ref[:, HEAD:]
                o_ref[turn, :, lanes] = (acc_ref[:, :HEAD] / total).astype(o_ref.dtype)
                l_ref[pl.ds(h, 1), pl.ds(start, BLOCK)] = eye_rows(top_ref[...] + jnp.log2(total))
                return 0

            lax.fori_loop(0, heads, one_head, 0)
            o_copy(turn).start()
            o_copy(turn).wait()
            return 0

        lax.fori_loop(0, turns, every, 0)

    owners, _, piece = send_ref.shape
    for o in range(owners):
        found = jnp.zeros(send_ref.shape[1:], jnp.float32)
        for j in range(tok // piece):
            found = jnp.where(owner_ref[j] == o, l_ref[:, j * piece : (j + 1) * piece] * LN2, found)
        send_ref[o] = found


def rest_part(owner, queries, lown, kv, old, done, owners, piece):
    tok, width = queries.shape
    size = len(old)
    heads = width // HEAD
    groups = old[0].shape[1] // HEAD
    turns = tok // BLOCK

    def kernel(*refs):
        rest_kernel(size, *refs)

    return pl.pallas_call(
        kernel,
        in_specs=[IN_SMEM, IN_HBM, IN_VMEM, IN_VMEM] + [IN_VMEM] * size + [IN_HBM],
        out_specs=(IN_HBM, IN_VMEM),
        out_shape=(
            jax.ShapeDtypeStruct((tok, width), jnp.bfloat16),
            jax.ShapeDtypeStruct((owners, heads, piece), jnp.float32),
        ),
        input_output_aliases={4 + size: 0},
        scratch_shapes=[
            pltpu.VMEM((turns, BLOCK, width), jnp.bfloat16),
            pltpu.VMEM((turns, BLOCK, width), jnp.bfloat16),
            pltpu.VMEM((groups, tok, HEAD), jnp.bfloat16),
            pltpu.VMEM((groups, tok, 2 * HEAD), jnp.bfloat16),
            pltpu.VMEM((heads, tok), jnp.float32),
            pltpu.VMEM((heads, tok), jnp.float32),
            pltpu.VMEM((BLOCK, 2 * HEAD), jnp.float32),
            pltpu.VMEM((BLOCK, HEAD), jnp.float32),
            pltpu.VMEM((1, tok), jnp.float32),
            pltpu.SemaphoreType.DMA((turns,)),
            pltpu.SemaphoreType.DMA((turns,)),
            pltpu.SemaphoreType.DMA((turns,)),
        ],
        compiler_params=pltpu.CompilerParams(vmem_limit_bytes=VMEM_LIMIT),
        cost_estimate=pl.CostEstimate(
            flops=tok * tok * width, bytes_accessed=4 * tok * width, transcendentals=tok * tok * heads // 4
        ),
    )(owner, queries, lown, kv, *old, done)


def spread_kernel(x_ref, o_ref):
    owners, _, piece = x_ref.shape
    for i in range(owners):
        o_ref[0, :, i * piece : (i + 1) * piece] = x_ref[i]


def spread(got):
    owners, heads, piece = got.shape
    return pl.pallas_call(
        spread_kernel,
        out_shape=jax.ShapeDtypeStruct((1, heads, owners * piece), got.dtype),
        cost_estimate=pl.CostEstimate(flops=0, bytes_accessed=8 * got.size, transcendentals=0),
    )(got)


def per_device(queries, keys, values, doc_ids, piece_owner):
    ctx_size, head_size = lax.axis_size("ctx"), lax.axis_size("head")
    tok, _ = queries.shape
    piece = 2 * tok // ctx_size

    own_send, *next_send = prep(keys, values, doc_ids.reshape(1, tok), head_size)
    kv = lax.all_to_all(own_send, "head", 0, 0, tiled=True)
    old = []
    for m in range(head_size):
        route = [
            (h * ctx_size + i, (h ^ m) * ctx_size + i + 1)
            for h in range(head_size)
            for i in range(ctx_size - 1)
        ]
        old.append(lax.ppermute(next_send[m], ("head", "ctx"), route))

    done, lown = own_part(queries, kv)
    attended, send = rest_part(piece_owner, queries, lown, kv, old, done, ctx_size, piece)
    got = lax.all_to_all(send, "ctx", 0, 0, tiled=True)
    return attended, spread(got)


def solution(mesh):
    return jax.shard_map(
        per_device,
        mesh=mesh,
        in_specs=(
            P("ctx", "head"),
            P("ctx", "head", None),
            P("ctx", "head", None),
            P("ctx"),
            P("ctx"),
        ),
        out_specs=(P("ctx", "head"), P("ctx", "head", None)),
        check_vma=False,
    )
```

```python
import itertools
import math

import jax
import jax.numpy as jnp
from jax import lax
from jax.experimental import pallas as pl
from jax.experimental.pallas import tpu as pltpu
from jax.sharding import PartitionSpec as P

HEAD = 128
BLOCK = 256
INFO = 16
CODE = 32
NEG = -1e30
FLOOR = 60.0
CEILING = 90.0
SCALE2 = HEAD ** (-0.5) * math.log2(math.e)
LN2 = math.log(2.0)
VMEM_LIMIT = 50 * 1024 * 1024
NT = (((1,), (1,)), ((), ()))
NN = (((1,), (0,)), ((), ()))
IN_VMEM = pl.BlockSpec(memory_space=pltpu.VMEM)
IN_SMEM = pl.BlockSpec(memory_space=pltpu.SMEM)
IN_HBM = pl.BlockSpec(memory_space=pltpu.HBM)


def f32_dot(a, b, dims):
    return lax.dot_general(a, b, dims, preferred_element_type=jnp.float32)


def eye_rows(column):
    eye = lax.broadcasted_iota(jnp.int32, (HEAD, HEAD), 0) == lax.broadcasted_iota(jnp.int32, (HEAD, HEAD), 1)
    parts = [
        jnp.sum(jnp.where(eye, column[i : i + HEAD], 0.0), axis=0, keepdims=True)
        for i in range(0, column.shape[0], HEAD)
    ]
    return jnp.concatenate(parts, axis=1)


def row_column(row):
    return jnp.broadcast_to(row, (HEAD, row.shape[1])).T


def count(flags):
    return jnp.sum(flags.astype(jnp.int32))


def tile_of(ref, turn):
    return ref.at[pl.ds(pl.multiple_of(turn * BLOCK, BLOCK), BLOCK), :]


def prep_kernel(size, k_ref, v_ref, docs_ref, own_ref, *next_refs):
    here = lax.axis_index("head")
    rows, cols = k_ref.shape[1], k_ref.shape[2] // size
    docs = docs_ref[...]
    last = docs[:, docs.shape[1] - 1 :]
    run = jnp.sum(jnp.where(docs == last, 1.0, 0.0), axis=1, keepdims=True)
    high = jnp.floor(run * (1.0 / CODE))
    line = lax.broadcasted_iota(jnp.int32, (INFO, cols), 0)
    info = jnp.where(line == 0, last.astype(jnp.float32), jnp.where(line == 1, high, run - high * CODE))
    info = info.astype(k_ref.dtype)
    ids = docs.astype(jnp.float32)
    table = jnp.zeros((INFO, cols), jnp.float32)
    for i in range(docs.shape[1] // cols):
        table = jnp.where(line == i, ids[:, i * cols : (i + 1) * cols], table)
    table = table.astype(k_ref.dtype)
    for j in range(size):
        own_ref[j, :rows] = k_ref[0, :, j * cols : (j + 1) * cols]
        own_ref[j, rows : 2 * rows] = v_ref[0, :, j * cols : (j + 1) * cols]
        own_ref[j, 2 * rows :] = table
    for m in range(size):
        start = pl.multiple_of(jnp.bitwise_xor(here, m) * cols, cols)
        next_refs[m][:rows] = k_ref[0, :, pl.ds(start, cols)]
        next_refs[m][rows : 2 * rows] = v_ref[0, :, pl.ds(start, cols)]
        next_refs[m][2 * rows :] = info


def prep(keys, values, docs, size):
    _, rows, width = keys.shape
    cols = width // size
    own = jax.ShapeDtypeStruct((size, 2 * rows + INFO, cols), keys.dtype)
    onward = jax.ShapeDtypeStruct((2 * rows + INFO, cols), keys.dtype)

    def kernel(*refs):
        prep_kernel(size, *refs)

    return pl.pallas_call(
        kernel,
        out_shape=(own,) + (onward,) * size,
        in_specs=[IN_VMEM] * 3,
        out_specs=(IN_VMEM,) * (size + 1),
        cost_estimate=pl.CostEstimate(flops=0, bytes_accessed=12 * keys.size, transcendentals=0),
    )(keys, values, docs)


def row_of_docs(kv_ref, tok):
    cols = kv_ref.shape[2]
    table = kv_ref[0, kv_ref.shape[1] - INFO :, :].astype(jnp.float32)
    return jnp.concatenate([table[i : i + 1] for i in range(tok // cols)], axis=1)


def own_kernel(q_ref, kv_ref, o_ref, l_ref, k_ref, vx_ref, bias_ref, docs_ref, first_ref):
    turn = pl.program_id(0)
    parts, rows = kv_ref.shape[0], (kv_ref.shape[1] - INFO) // 2
    groups = vx_ref.shape[0]
    tok = parts * rows
    turns = tok // BLOCK
    share = q_ref.shape[1] // HEAD // groups

    @pl.when(turn == 0)
    def _():
        docs = row_of_docs(kv_ref, tok)
        docs_ref[...] = docs
        for t in range(turns):
            first_ref[t] = count(docs < docs[:, t * BLOCK : t * BLOCK + 1]) // BLOCK
        for j in range(parts):
            span = slice(j * rows, (j + 1) * rows)
            k_ref[span] = kv_ref[j, :rows]
            for g in range(groups):
                vx_ref[g, span, :HEAD] = kv_ref[j, rows : 2 * rows, g * HEAD : (g + 1) * HEAD]
                vx_ref[g, span, HEAD:] = jnp.ones((rows, HEAD), vx_ref.dtype)

    first = first_ref[turn]
    for n in range(1, turns + 1):

        @pl.when(turn - first + 1 == n)
        def _(n=n):
            width = n * BLOCK
            base = pl.multiple_of(first * BLOCK, BLOCK)
            here = pl.multiple_of(turn * BLOCK, BLOCK)
            q_docs = row_column(docs_ref[:, pl.ds(here, BLOCK)])
            k_docs = docs_ref[:, pl.ds(base, width)]
            ahead = lax.broadcasted_iota(jnp.int32, (BLOCK, width), 1) - lax.broadcasted_iota(
                jnp.int32, (BLOCK, width), 0
            )
            keep = (jnp.concatenate([q_docs] * (width // HEAD), axis=1) == k_docs) & (ahead <= width - BLOCK)
            bias_ref[:, :width] = jnp.where(keep, 0.0, NEG)
            for h in range(groups * share):
                g = h // share
                lanes = slice(h * HEAD, (h + 1) * HEAD)
                k = k_ref[pl.ds(base, width), g * HEAD : (g + 1) * HEAD]
                s = f32_dot(q_ref[:, lanes], k, NT) * SCALE2 + bias_ref[:, :width]
                got = f32_dot(jnp.exp2(s).astype(jnp.bfloat16), vx_ref[g, pl.ds(base, width), :], NN)
                total = got[:, HEAD:]
                o_ref[:, lanes] = (got[:, :HEAD] / total).astype(o_ref.dtype)
                l_ref[h : h + 1, :] = eye_rows(jnp.log2(total))


def own_part(queries, kv):
    tok, width = queries.shape
    groups = kv.shape[2] // HEAD
    return pl.pallas_call(
        own_kernel,
        grid=(tok // BLOCK,),
        in_specs=[
            pl.BlockSpec((BLOCK, width), lambda t: (t, 0)),
            pl.BlockSpec(kv.shape, lambda t: (0, 0, 0)),
        ],
        out_specs=(
            pl.BlockSpec((BLOCK, width), lambda t: (t, 0)),
            pl.BlockSpec((width // HEAD, BLOCK), lambda t: (0, t)),
        ),
        out_shape=(
            jax.ShapeDtypeStruct((tok, width), jnp.bfloat16),
            jax.ShapeDtypeStruct((width // HEAD, tok), jnp.float32),
        ),
        scratch_shapes=[
            pltpu.VMEM((tok, groups * HEAD), jnp.bfloat16),
            pltpu.VMEM((groups, tok, 2 * HEAD), jnp.bfloat16),
            pltpu.VMEM((BLOCK, tok), jnp.float32),
            pltpu.VMEM((1, tok), jnp.float32),
            pltpu.SMEM((tok // BLOCK,), jnp.int32),
        ],
        compiler_params=pltpu.CompilerParams(vmem_limit_bytes=VMEM_LIMIT),
        cost_estimate=pl.CostEstimate(
            flops=4 * tok * tok * width, bytes_accessed=4 * tok * width, transcendentals=tok * tok * width // HEAD // 2
        ),
    )(queries, kv)


def beyond(logs):
    return jnp.logical_not((logs > -FLOOR) & (logs < CEILING))


def rest_kernel(size, owner_ref, q_hbm, lown_ref, kv_ref, *refs):
    old_refs = refs[:size]
    done_hbm, o_hbm, send_ref, q_ref, o_ref, k_ref, vx_ref, new_ref, l_ref, acc_ref, top_ref = refs[size : size + 11]
    docs_ref, q_sem, d_sem, o_sem = refs[size + 11 :]
    del done_hbm
    turns = q_ref.shape[0]
    groups = vx_ref.shape[0]
    heads = q_ref.shape[2] // HEAD
    share = heads // groups
    rows = (old_refs[0].shape[0] - INFO) // 2
    tok = turns * BLOCK

    def q_copy(turn):
        return pltpu.make_async_copy(tile_of(q_hbm, turn), q_ref.at[turn], q_sem.at[turn])

    def d_copy(turn):
        return pltpu.make_async_copy(tile_of(o_hbm, turn), o_ref.at[turn], d_sem.at[turn])

    def o_copy(turn):
        return pltpu.make_async_copy(o_ref.at[turn], tile_of(o_hbm, turn), o_sem.at[turn])

    q_copy(0).start()
    d_copy(0).start()
    info = old_refs[0][2 * rows :, :HEAD].astype(jnp.float32)
    docs = row_of_docs(kv_ref, tok)
    same = info[0:1] == docs[:, :1]
    ahead = jnp.max(jnp.where(same, info[1:2] * CODE + info[2:3], 0.0)).astype(jnp.int32)
    behind = count(docs == docs[:, :1])
    steps = jnp.where(ahead > 0, (behind + BLOCK - 1) // BLOCK, 0)

    for turn in range(1, turns):

        @pl.when(turn < steps)
        def _(turn=turn):
            q_copy(turn).start()
            d_copy(turn).start()

    new_ref[...] = jnp.zeros(new_ref.shape, jnp.float32)
    here = lax.axis_index("head")
    for m in range(size):
        base = pl.multiple_of(jnp.bitwise_xor(here, m) * rows, rows)
        for g in range(groups):
            lanes = slice(g * HEAD, (g + 1) * HEAD)
            k_ref[g, pl.ds(base, rows), :] = old_refs[m][:rows, lanes]
            vx_ref[g, pl.ds(base, rows), :HEAD] = old_refs[m][rows : 2 * rows, lanes]
            vx_ref[g, pl.ds(base, rows), HEAD:] = jnp.ones((rows, HEAD), vx_ref.dtype)

    def one(turn, _):
        q_copy(turn).wait()
        d_copy(turn).wait()
        start = pl.multiple_of(turn * BLOCK, BLOCK)
        short = behind - start <= BLOCK // 2
        for n, tall in itertools.product(range(1, turns + 1), (BLOCK // 2, BLOCK)):

            @pl.when(((ahead + BLOCK - 1) // BLOCK == n) & (short == (tall < BLOCK)))
            def _(n=n, tall=tall):
                width = n * BLOCK
                inside = start + lax.broadcasted_iota(jnp.int32, (tall, HEAD), 0) < behind
                place = lax.broadcasted_iota(jnp.int32, (1, width), 1)
                bias = jnp.where(place >= width - ahead, 0.0, NEG)

                for g in range(groups):
                    k = k_ref[g, tok - width :, :]
                    vx = vx_ref[g, tok - width :, :]
                    top_head = g * share
                    weights = jnp.exp2(lown_ref[pl.ds(top_head, share), pl.ds(start, tall)])
                    found = []
                    for h in range(share):
                        lanes = slice((g * share + h) * HEAD, (g * share + h + 1) * HEAD)
                        s = f32_dot(q_ref[turn, :tall, lanes], k, NT) * SCALE2 + bias
                        got = f32_dot(jnp.exp2(s).astype(jnp.bfloat16), vx, NN)
                        total = jnp.where(inside, got[:, HEAD:], 0.0)
                        before = o_ref[turn, :tall, lanes].astype(jnp.float32)
                        weight = row_column(weights[h : h + 1])
                        mixed = (before * weight + got[:, :HEAD]) / (weight + total)
                        o_ref[turn, :tall, lanes] = jnp.where(inside, mixed, before).astype(o_ref.dtype)
                        found.append(eye_rows(total))
                    new_ref[pl.ds(top_head, share), pl.ds(start, tall)] = jnp.concatenate(found, axis=0)

        o_copy(turn).start()
        return 0

    lax.fori_loop(0, steps, one, 0)

    @pl.when(steps == 0)
    def _():
        q_copy(0).wait()
        d_copy(0).wait()

    own = lown_ref[...]
    new = new_ref[...]
    l_ref[...] = jnp.log2(jnp.exp2(own) + new)
    token = lax.broadcasted_iota(jnp.int32, (heads, tok), 1)
    met = (token < behind) & (ahead > 0)
    bad = count(beyond(own) | (met & beyond(jnp.log2(new))))
    for turn in range(turns):

        @pl.when(turn < steps)
        def _(turn=turn):
            o_copy(turn).wait()

    @pl.when(bad > 0)
    def _():
        docs_ref[...] = docs

        def every(turn, _):
            q_copy(turn).start()
            q_copy(turn).wait()
            start = pl.multiple_of(turn * BLOCK, BLOCK)
            q_docs = row_column(docs_ref[:, pl.ds(start, BLOCK)])
            q_docs = jnp.concatenate([q_docs] * (BLOCK // HEAD), axis=1)
            row = start + lax.broadcasted_iota(jnp.int32, (BLOCK, BLOCK), 0)
            column = lax.broadcasted_iota(jnp.int32, (BLOCK, BLOCK), 1)

            def one_head(h, _):
                g = h // share
                lanes = pl.ds(pl.multiple_of(h * HEAD, HEAD), HEAD)
                q = q_ref[turn, :, lanes]
                acc_ref[...] = jnp.zeros(acc_ref.shape, jnp.float32)
                top_ref[...] = jnp.full(top_ref.shape, NEG, jnp.float32)

                def add(keep, k, v):
                    s = jnp.where(keep, f32_dot(q, k, NT) * SCALE2, NEG)
                    before = top_ref[...]
                    top = jnp.maximum(before, jnp.max(s, axis=1, keepdims=True))
                    shift = jnp.exp2(before - top)
                    p = jnp.where(keep, jnp.exp2(s - jnp.concatenate([top] * (BLOCK // HEAD), axis=1)), 0.0)
                    p = p.astype(jnp.bfloat16)
                    ones = jnp.ones(v.shape, v.dtype)
                    acc_ref[:, :HEAD] = acc_ref[:, :HEAD] * shift + f32_dot(p, v, NN)
                    acc_ref[:, HEAD:] = acc_ref[:, HEAD:] * shift + f32_dot(p, ones, NN)
                    top_ref[...] = top

                def old_block(j, _):
                    at = pl.multiple_of(j * BLOCK, BLOCK)
                    keep = (j * BLOCK + column >= tok - ahead) & (row < behind)
                    add(keep, k_ref[g, pl.ds(at, BLOCK), :], vx_ref[g, pl.ds(at, BLOCK), :HEAD])
                    return 0

                def own_block(j, _):
                    at = pl.multiple_of(j * BLOCK, BLOCK)
                    keep = (q_docs == docs_ref[:, pl.ds(at, BLOCK)]) & (j * BLOCK + column <= row)
                    per = BLOCK // rows
                    group = pl.ds(pl.multiple_of(g * HEAD, HEAD), HEAD)
                    k = jnp.concatenate([kv_ref[j * per + i, :rows, group] for i in range(per)], axis=0)
                    v = jnp.concatenate([kv_ref[j * per + i, rows : 2 * rows, group] for i in range(per)], axis=0)
                    add(keep, k, v)
                    return 0

                lax.fori_loop(0, turns, old_block, 0)
                lax.fori_loop(0, turn + 1, own_block, 0)
                total = acc_ref[:, HEAD:]
                o_ref[turn, :, lanes] = (acc_ref[:, :HEAD] / total).astype(o_ref.dtype)
                l_ref[pl.ds(h, 1), pl.ds(start, BLOCK)] = eye_rows(top_ref[...] + jnp.log2(total))
                return 0

            lax.fori_loop(0, heads, one_head, 0)
            o_copy(turn).start()
            o_copy(turn).wait()
            return 0

        lax.fori_loop(0, turns, every, 0)

    owners, _, piece = send_ref.shape
    for o in range(owners):
        found = jnp.zeros(send_ref.shape[1:], jnp.float32)
        for j in range(tok // piece):
            found = jnp.where(owner_ref[j] == o, l_ref[:, j * piece : (j + 1) * piece] * LN2, found)
        send_ref[o] = found


def rest_part(owner, queries, lown, kv, old, done, owners, piece):
    tok, width = queries.shape
    size = len(old)
    heads = width // HEAD
    groups = old[0].shape[1] // HEAD
    turns = tok // BLOCK

    def kernel(*refs):
        rest_kernel(size, *refs)

    return pl.pallas_call(
        kernel,
        in_specs=[IN_SMEM, IN_HBM, IN_VMEM, IN_VMEM] + [IN_VMEM] * size + [IN_HBM],
        out_specs=(IN_HBM, IN_VMEM),
        out_shape=(
            jax.ShapeDtypeStruct((tok, width), jnp.bfloat16),
            jax.ShapeDtypeStruct((owners, heads, piece), jnp.float32),
        ),
        input_output_aliases={4 + size: 0},
        scratch_shapes=[
            pltpu.VMEM((turns, BLOCK, width), jnp.bfloat16),
            pltpu.VMEM((turns, BLOCK, width), jnp.bfloat16),
            pltpu.VMEM((groups, tok, HEAD), jnp.bfloat16),
            pltpu.VMEM((groups, tok, 2 * HEAD), jnp.bfloat16),
            pltpu.VMEM((heads, tok), jnp.float32),
            pltpu.VMEM((heads, tok), jnp.float32),
            pltpu.VMEM((BLOCK, 2 * HEAD), jnp.float32),
            pltpu.VMEM((BLOCK, HEAD), jnp.float32),
            pltpu.VMEM((1, tok), jnp.float32),
            pltpu.SemaphoreType.DMA((turns,)),
            pltpu.SemaphoreType.DMA((turns,)),
            pltpu.SemaphoreType.DMA((turns,)),
        ],
        compiler_params=pltpu.CompilerParams(vmem_limit_bytes=VMEM_LIMIT),
        cost_estimate=pl.CostEstimate(
            flops=tok * tok * width, bytes_accessed=4 * tok * width, transcendentals=tok * tok * heads // 4
        ),
    )(owner, queries, lown, kv, *old, done)


def spread_kernel(x_ref, o_ref):
    owners, _, piece = x_ref.shape
    for i in range(owners):
        o_ref[0, :, i * piece : (i + 1) * piece] = x_ref[i]


def spread(got):
    owners, heads, piece = got.shape
    return pl.pallas_call(
        spread_kernel,
        out_shape=jax.ShapeDtypeStruct((1, heads, owners * piece), got.dtype),
        cost_estimate=pl.CostEstimate(flops=0, bytes_accessed=8 * got.size, transcendentals=0),
    )(got)


def per_device(queries, keys, values, doc_ids, piece_owner):
    ctx_size, head_size = lax.axis_size("ctx"), lax.axis_size("head")
    tok, _ = queries.shape
    piece = 2 * tok // ctx_size

    own_send, *next_send = prep(keys, values, doc_ids.reshape(1, tok), head_size)
    kv = lax.all_to_all(own_send, "head", 0, 0, tiled=True)
    old = []
    for m in range(head_size):
        route = [
            (h * ctx_size + i, (h ^ m) * ctx_size + i + 1)
            for h in range(head_size)
            for i in range(ctx_size - 1)
        ]
        old.append(lax.ppermute(next_send[m], ("head", "ctx"), route))

    done, lown = own_part(queries, kv)
    attended, send = rest_part(piece_owner, queries, lown, kv, old, done, ctx_size, piece)
    got = lax.all_to_all(send, "ctx", 0, 0, tiled=True)
    return attended, spread(got)


def solution(mesh):
    return jax.shard_map(
        per_device,
        mesh=mesh,
        in_specs=(
            P("ctx", "head"),
            P("ctx", "head", None),
            P("ctx", "head", None),
            P("ctx"),
            P("ctx"),
        ),
        out_specs=(P("ctx", "head"), P("ctx", "head", None)),
        check_vma=False,
    )
```

```python
import itertools
import math

import jax
import jax.numpy as jnp
from jax import lax
from jax.experimental import pallas as pl
from jax.experimental.pallas import tpu as pltpu
from jax.sharding import PartitionSpec as P

HEAD = 128
BLOCK = 256
INFO = 16
CODE = 32
NEG = -1e30
FLOOR = 60.0
CEILING = 90.0
SCALE2 = HEAD ** (-0.5) * math.log2(math.e)
LN2 = math.log(2.0)
VMEM_LIMIT = 50 * 1024 * 1024
NT = (((1,), (1,)), ((), ()))
NN = (((1,), (0,)), ((), ()))
IN_VMEM = pl.BlockSpec(memory_space=pltpu.VMEM)
IN_SMEM = pl.BlockSpec(memory_space=pltpu.SMEM)
IN_HBM = pl.BlockSpec(memory_space=pltpu.HBM)


def f32_dot(a, b, dims):
    return lax.dot_general(a, b, dims, preferred_element_type=jnp.float32)


def eye_rows(column):
    eye = lax.broadcasted_iota(jnp.int32, (HEAD, HEAD), 0) == lax.broadcasted_iota(jnp.int32, (HEAD, HEAD), 1)
    parts = [
        jnp.sum(jnp.where(eye, column[i : i + HEAD], 0.0), axis=0, keepdims=True)
        for i in range(0, column.shape[0], HEAD)
    ]
    return jnp.concatenate(parts, axis=1)


def row_column(row):
    return jnp.broadcast_to(row, (HEAD, row.shape[1])).T


def count(flags):
    return jnp.sum(flags.astype(jnp.int32))


def tile_of(ref, turn):
    return ref.at[pl.ds(pl.multiple_of(turn * BLOCK, BLOCK), BLOCK), :]


def prep_kernel(size, k_ref, v_ref, docs_ref, own_ref, *next_refs):
    here = lax.axis_index("head")
    rows, cols = k_ref.shape[1], k_ref.shape[2] // size
    docs = docs_ref[...]
    last = docs[:, docs.shape[1] - 1 :]
    run = jnp.sum(jnp.where(docs == last, 1.0, 0.0), axis=1, keepdims=True)
    high = jnp.floor(run * (1.0 / CODE))
    line = lax.broadcasted_iota(jnp.int32, (INFO, cols), 0)
    info = jnp.where(line == 0, last.astype(jnp.float32), jnp.where(line == 1, high, run - high * CODE))
    info = info.astype(k_ref.dtype)
    ids = docs.astype(jnp.float32)
    table = jnp.zeros((INFO, cols), jnp.float32)
    for i in range(docs.shape[1] // cols):
        table = jnp.where(line == i, ids[:, i * cols : (i + 1) * cols], table)
    table = table.astype(k_ref.dtype)
    for j in range(size):
        own_ref[j, :rows] = k_ref[0, :, j * cols : (j + 1) * cols]
        own_ref[j, rows : 2 * rows] = v_ref[0, :, j * cols : (j + 1) * cols]
        own_ref[j, 2 * rows :] = table
    for m in range(size):
        start = pl.multiple_of(jnp.bitwise_xor(here, m) * cols, cols)
        next_refs[m][:rows] = k_ref[0, :, pl.ds(start, cols)]
        next_refs[m][rows : 2 * rows] = v_ref[0, :, pl.ds(start, cols)]
        next_refs[m][2 * rows :] = info


def prep(keys, values, docs, size):
    _, rows, width = keys.shape
    cols = width // size
    own = jax.ShapeDtypeStruct((size, 2 * rows + INFO, cols), keys.dtype)
    onward = jax.ShapeDtypeStruct((2 * rows + INFO, cols), keys.dtype)

    def kernel(*refs):
        prep_kernel(size, *refs)

    return pl.pallas_call(
        kernel,
        out_shape=(own,) + (onward,) * size,
        in_specs=[IN_VMEM] * 3,
        out_specs=(IN_VMEM,) * (size + 1),
        cost_estimate=pl.CostEstimate(flops=0, bytes_accessed=12 * keys.size, transcendentals=0),
    )(keys, values, docs)


def row_of_docs(kv_ref, tok):
    cols = kv_ref.shape[2]
    table = kv_ref[0, kv_ref.shape[1] - INFO :, :].astype(jnp.float32)
    return jnp.concatenate([table[i : i + 1] for i in range(tok // cols)], axis=1)


def own_kernel(q_ref, kv_ref, o_ref, l_ref, k_ref, vx_ref, bias_ref, docs_ref, first_ref):
    turn = pl.program_id(0)
    parts, rows = kv_ref.shape[0], (kv_ref.shape[1] - INFO) // 2
    groups = vx_ref.shape[0]
    tok = parts * rows
    turns = tok // BLOCK
    share = q_ref.shape[1] // HEAD // groups

    @pl.when(turn == 0)
    def _():
        docs = row_of_docs(kv_ref, tok)
        docs_ref[...] = docs
        for t in range(turns):
            first_ref[t] = count(docs < docs[:, t * BLOCK : t * BLOCK + 1]) // BLOCK
        for j in range(parts):
            span = slice(j * rows, (j + 1) * rows)
            k_ref[span] = kv_ref[j, :rows]
            for g in range(groups):
                vx_ref[g, span, :HEAD] = kv_ref[j, rows : 2 * rows, g * HEAD : (g + 1) * HEAD]
                vx_ref[g, span, HEAD:] = jnp.ones((rows, HEAD), vx_ref.dtype)

    first = first_ref[turn]
    for n in range(1, turns + 1):

        @pl.when(turn - first + 1 == n)
        def _(n=n):
            width = n * BLOCK
            base = pl.multiple_of(first * BLOCK, BLOCK)
            here = pl.multiple_of(turn * BLOCK, BLOCK)
            q_docs = row_column(docs_ref[:, pl.ds(here, BLOCK)])
            k_docs = docs_ref[:, pl.ds(base, width)]
            keep = jnp.concatenate([q_docs] * (width // HEAD), axis=1) == k_docs
            past = lax.broadcasted_iota(jnp.int32, (BLOCK, BLOCK), 1) <= lax.broadcasted_iota(
                jnp.int32, (BLOCK, BLOCK), 0
            )
            if n > 1:
                bias_ref[:, : width - BLOCK] = jnp.where(keep[:, : width - BLOCK], 0.0, NEG)
            bias_ref[:, width - BLOCK : width] = jnp.where(keep[:, width - BLOCK :] & past, 0.0, NEG)
            for h in range(groups * share):
                g = h // share
                lanes = slice(h * HEAD, (h + 1) * HEAD)
                k = k_ref[pl.ds(base, width), g * HEAD : (g + 1) * HEAD]
                s = f32_dot(q_ref[:, lanes], k, NT) * SCALE2 + bias_ref[:, :width]
                got = f32_dot(jnp.exp2(s).astype(jnp.bfloat16), vx_ref[g, pl.ds(base, width), :], NN)
                total = got[:, HEAD:]
                o_ref[:, lanes] = (got[:, :HEAD] / total).astype(o_ref.dtype)
                l_ref[h : h + 1, :] = eye_rows(jnp.log2(total))


def own_part(queries, kv):
    tok, width = queries.shape
    groups = kv.shape[2] // HEAD
    return pl.pallas_call(
        own_kernel,
        grid=(tok // BLOCK,),
        in_specs=[
            pl.BlockSpec((BLOCK, width), lambda t: (t, 0)),
            IN_VMEM,
        ],
        out_specs=(
            pl.BlockSpec((BLOCK, width), lambda t: (t, 0)),
            pl.BlockSpec((width // HEAD, BLOCK), lambda t: (0, t)),
        ),
        out_shape=(
            jax.ShapeDtypeStruct((tok, width), jnp.bfloat16),
            jax.ShapeDtypeStruct((width // HEAD, tok), jnp.float32),
        ),
        scratch_shapes=[
            pltpu.VMEM((tok, groups * HEAD), jnp.bfloat16),
            pltpu.VMEM((groups, tok, 2 * HEAD), jnp.bfloat16),
            pltpu.VMEM((BLOCK, tok), jnp.float32),
            pltpu.VMEM((1, tok), jnp.float32),
            pltpu.SMEM((tok // BLOCK,), jnp.int32),
        ],
        compiler_params=pltpu.CompilerParams(vmem_limit_bytes=VMEM_LIMIT),
        cost_estimate=pl.CostEstimate(
            flops=4 * tok * tok * width, bytes_accessed=4 * tok * width, transcendentals=tok * tok * width // HEAD // 2
        ),
    )(queries, kv)


def beyond(logs):
    return jnp.logical_not((logs > -FLOOR) & (logs < CEILING))


def rest_kernel(size, owner_ref, q_hbm, lown_ref, kv_ref, *refs):
    old_refs = refs[:size]
    done_hbm, o_hbm, send_ref, q_ref, o_ref, k_ref, vx_ref, new_ref, l_ref, acc_ref, top_ref = refs[size : size + 11]
    docs_ref, q_sem, d_sem, o_sem = refs[size + 11 :]
    del done_hbm
    turns = q_ref.shape[0]
    groups = vx_ref.shape[0]
    heads = q_ref.shape[2] // HEAD
    share = heads // groups
    rows = (old_refs[0].shape[0] - INFO) // 2
    tok = turns * BLOCK

    def q_copy(turn):
        return pltpu.make_async_copy(tile_of(q_hbm, turn), q_ref.at[turn], q_sem.at[turn])

    def d_copy(turn):
        return pltpu.make_async_copy(tile_of(o_hbm, turn), o_ref.at[turn], d_sem.at[turn])

    def o_copy(turn):
        return pltpu.make_async_copy(o_ref.at[turn], tile_of(o_hbm, turn), o_sem.at[turn])

    q_copy(0).start()
    d_copy(0).start()
    info = old_refs[0][2 * rows :, :HEAD].astype(jnp.float32)
    docs = row_of_docs(kv_ref, tok)
    same = info[0:1] == docs[:, :1]
    ahead = jnp.max(jnp.where(same, info[1:2] * CODE + info[2:3], 0.0)).astype(jnp.int32)
    behind = count(docs == docs[:, :1])
    steps = jnp.where(ahead > 0, (behind + BLOCK - 1) // BLOCK, 0)

    for turn in range(1, turns):

        @pl.when(turn < steps)
        def _(turn=turn):
            q_copy(turn).start()
            d_copy(turn).start()

    new_ref[...] = jnp.zeros(new_ref.shape, jnp.float32)
    here = lax.axis_index("head")
    for m in range(size):
        base = pl.multiple_of(jnp.bitwise_xor(here, m) * rows, rows)
        for g in range(groups):
            lanes = slice(g * HEAD, (g + 1) * HEAD)
            k_ref[g, pl.ds(base, rows), :] = old_refs[m][:rows, lanes]
            vx_ref[g, pl.ds(base, rows), :HEAD] = old_refs[m][rows : 2 * rows, lanes]
            vx_ref[g, pl.ds(base, rows), HEAD:] = jnp.ones((rows, HEAD), vx_ref.dtype)

    def one(turn, _):
        q_copy(turn).wait()
        d_copy(turn).wait()
        start = pl.multiple_of(turn * BLOCK, BLOCK)
        short = behind - start <= BLOCK // 2
        for n, tall in itertools.product(range(1, turns + 1), (BLOCK // 2, BLOCK)):

            @pl.when(((ahead + BLOCK - 1) // BLOCK == n) & (short == (tall < BLOCK)))
            def _(n=n, tall=tall):
                width = n * BLOCK
                inside = start + lax.broadcasted_iota(jnp.int32, (tall, HEAD), 0) < behind
                place = lax.broadcasted_iota(jnp.int32, (1, width), 1)
                bias = jnp.where(place >= width - ahead, 0.0, NEG)

                for g in range(groups):
                    k = k_ref[g, tok - width :, :]
                    vx = vx_ref[g, tok - width :, :]
                    top_head = g * share
                    weights = jnp.exp2(lown_ref[pl.ds(top_head, share), pl.ds(start, tall)])
                    found = []
                    for h in range(share):
                        lanes = slice((g * share + h) * HEAD, (g * share + h + 1) * HEAD)
                        s = f32_dot(q_ref[turn, :tall, lanes], k, NT) * SCALE2 + bias
                        got = f32_dot(jnp.exp2(s).astype(jnp.bfloat16), vx, NN)
                        total = jnp.where(inside, got[:, HEAD:], 0.0)
                        before = o_ref[turn, :tall, lanes].astype(jnp.float32)
                        weight = row_column(weights[h : h + 1])
                        mixed = (before * weight + got[:, :HEAD]) / (weight + total)
                        o_ref[turn, :tall, lanes] = jnp.where(inside, mixed, before).astype(o_ref.dtype)
                        found.append(eye_rows(total))
                    new_ref[pl.ds(top_head, share), pl.ds(start, tall)] = jnp.concatenate(found, axis=0)

        o_copy(turn).start()
        return 0

    lax.fori_loop(0, steps, one, 0)

    @pl.when(steps == 0)
    def _():
        q_copy(0).wait()
        d_copy(0).wait()

    own = lown_ref[...]
    new = new_ref[...]
    l_ref[...] = jnp.log2(jnp.exp2(own) + new)
    token = lax.broadcasted_iota(jnp.int32, (heads, tok), 1)
    met = (token < behind) & (ahead > 0)
    bad = count(beyond(own) | (met & beyond(jnp.log2(new))))
    def wait_for_rows():
        for turn in range(turns):

            @pl.when(turn < steps)
            def _(turn=turn):
                o_copy(turn).wait()

    @pl.when(bad > 0)
    def _():
        wait_for_rows()
        docs_ref[...] = docs

        def every(turn, _):
            q_copy(turn).start()
            q_copy(turn).wait()
            start = pl.multiple_of(turn * BLOCK, BLOCK)
            q_docs = row_column(docs_ref[:, pl.ds(start, BLOCK)])
            q_docs = jnp.concatenate([q_docs] * (BLOCK // HEAD), axis=1)
            row = start + lax.broadcasted_iota(jnp.int32, (BLOCK, BLOCK), 0)
            column = lax.broadcasted_iota(jnp.int32, (BLOCK, BLOCK), 1)

            def one_head(h, _):
                g = h // share
                lanes = pl.ds(pl.multiple_of(h * HEAD, HEAD), HEAD)
                q = q_ref[turn, :, lanes]
                acc_ref[...] = jnp.zeros(acc_ref.shape, jnp.float32)
                top_ref[...] = jnp.full(top_ref.shape, NEG, jnp.float32)

                def add(keep, k, v):
                    s = jnp.where(keep, f32_dot(q, k, NT) * SCALE2, NEG)
                    before = top_ref[...]
                    top = jnp.maximum(before, jnp.max(s, axis=1, keepdims=True))
                    shift = jnp.exp2(before - top)
                    p = jnp.where(keep, jnp.exp2(s - jnp.concatenate([top] * (BLOCK // HEAD), axis=1)), 0.0)
                    p = p.astype(jnp.bfloat16)
                    ones = jnp.ones(v.shape, v.dtype)
                    acc_ref[:, :HEAD] = acc_ref[:, :HEAD] * shift + f32_dot(p, v, NN)
                    acc_ref[:, HEAD:] = acc_ref[:, HEAD:] * shift + f32_dot(p, ones, NN)
                    top_ref[...] = top

                def old_block(j, _):
                    at = pl.multiple_of(j * BLOCK, BLOCK)
                    keep = (j * BLOCK + column >= tok - ahead) & (row < behind)
                    add(keep, k_ref[g, pl.ds(at, BLOCK), :], vx_ref[g, pl.ds(at, BLOCK), :HEAD])
                    return 0

                def own_block(j, _):
                    at = pl.multiple_of(j * BLOCK, BLOCK)
                    keep = (q_docs == docs_ref[:, pl.ds(at, BLOCK)]) & (j * BLOCK + column <= row)
                    per = BLOCK // rows
                    group = pl.ds(pl.multiple_of(g * HEAD, HEAD), HEAD)
                    k = jnp.concatenate([kv_ref[j * per + i, :rows, group] for i in range(per)], axis=0)
                    v = jnp.concatenate([kv_ref[j * per + i, rows : 2 * rows, group] for i in range(per)], axis=0)
                    add(keep, k, v)
                    return 0

                lax.fori_loop(0, turns, old_block, 0)
                lax.fori_loop(0, turn + 1, own_block, 0)
                total = acc_ref[:, HEAD:]
                o_ref[turn, :, lanes] = (acc_ref[:, :HEAD] / total).astype(o_ref.dtype)
                l_ref[pl.ds(h, 1), pl.ds(start, BLOCK)] = eye_rows(top_ref[...] + jnp.log2(total))
                return 0

            lax.fori_loop(0, heads, one_head, 0)
            o_copy(turn).start()
            o_copy(turn).wait()
            return 0

        lax.fori_loop(0, turns, every, 0)

    owners, _, piece = send_ref.shape
    for o in range(owners):
        found = jnp.zeros(send_ref.shape[1:], jnp.float32)
        for j in range(tok // piece):
            found = jnp.where(owner_ref[j] == o, l_ref[:, j * piece : (j + 1) * piece] * LN2, found)
        send_ref[o] = found

    @pl.when(bad == 0)
    def _():
        wait_for_rows()


def rest_part(owner, queries, lown, kv, old, done, owners, piece):
    tok, width = queries.shape
    size = len(old)
    heads = width // HEAD
    groups = old[0].shape[1] // HEAD
    turns = tok // BLOCK

    def kernel(*refs):
        rest_kernel(size, *refs)

    return pl.pallas_call(
        kernel,
        in_specs=[IN_SMEM, IN_HBM, IN_VMEM, IN_VMEM] + [IN_VMEM] * size + [IN_HBM],
        out_specs=(IN_HBM, IN_VMEM),
        out_shape=(
            jax.ShapeDtypeStruct((tok, width), jnp.bfloat16),
            jax.ShapeDtypeStruct((owners, heads, piece), jnp.float32),
        ),
        input_output_aliases={4 + size: 0},
        scratch_shapes=[
            pltpu.VMEM((turns, BLOCK, width), jnp.bfloat16),
            pltpu.VMEM((turns, BLOCK, width), jnp.bfloat16),
            pltpu.VMEM((groups, tok, HEAD), jnp.bfloat16),
            pltpu.VMEM((groups, tok, 2 * HEAD), jnp.bfloat16),
            pltpu.VMEM((heads, tok), jnp.float32),
            pltpu.VMEM((heads, tok), jnp.float32),
            pltpu.VMEM((BLOCK, 2 * HEAD), jnp.float32),
            pltpu.VMEM((BLOCK, HEAD), jnp.float32),
            pltpu.VMEM((1, tok), jnp.float32),
            pltpu.SemaphoreType.DMA((turns,)),
            pltpu.SemaphoreType.DMA((turns,)),
            pltpu.SemaphoreType.DMA((turns,)),
        ],
        compiler_params=pltpu.CompilerParams(vmem_limit_bytes=VMEM_LIMIT),
        cost_estimate=pl.CostEstimate(
            flops=tok * tok * width, bytes_accessed=4 * tok * width, transcendentals=tok * tok * heads // 4
        ),
    )(owner, queries, lown, kv, *old, done)


def spread_kernel(x_ref, o_ref):
    owners, _, piece = x_ref.shape
    for i in range(owners):
        o_ref[0, :, i * piece : (i + 1) * piece] = x_ref[i]


def spread(got):
    owners, heads, piece = got.shape
    return pl.pallas_call(
        spread_kernel,
        out_shape=jax.ShapeDtypeStruct((1, heads, owners * piece), got.dtype),
        cost_estimate=pl.CostEstimate(flops=0, bytes_accessed=8 * got.size, transcendentals=0),
    )(got)


def per_device(queries, keys, values, doc_ids, piece_owner):
    ctx_size, head_size = lax.axis_size("ctx"), lax.axis_size("head")
    tok, _ = queries.shape
    piece = 2 * tok // ctx_size

    own_send, *next_send = prep(keys, values, doc_ids.reshape(1, tok), head_size)
    kv = lax.all_to_all(own_send, "head", 0, 0, tiled=True)
    old = []
    for m in range(head_size):
        route = [
            (h * ctx_size + i, (h ^ m) * ctx_size + i + 1)
            for h in range(head_size)
            for i in range(ctx_size - 1)
        ]
        old.append(lax.ppermute(next_send[m], ("head", "ctx"), route))

    done, lown = own_part(queries, kv)
    attended, send = rest_part(piece_owner, queries, lown, kv, old, done, ctx_size, piece)
    got = lax.all_to_all(send, "ctx", 0, 0, tiled=True)
    return attended, spread(got)


def solution(mesh):
    return jax.shard_map(
        per_device,
        mesh=mesh,
        in_specs=(
            P("ctx", "head"),
            P("ctx", "head", None),
            P("ctx", "head", None),
            P("ctx"),
            P("ctx"),
        ),
        out_specs=(P("ctx", "head"), P("ctx", "head", None)),
        check_vma=False,
    )
```
